512 devices in a mesh: ctx: 32 (over z, core), exp: 16 (over x, y).
Axes of the slice: x: 4, y: 4, z: 16, core: 2. Of those that a mesh axis runs over, the one named last changes fastest.
Arguments:
- seq_x: bfloat16 [4096, 5120], P('ctx', 'exp'), may hold values from -6 to 6
- z_gate: bfloat16 [4096, 5120], P('ctx', 'exp'), may hold values from -6 to 6
- bc_in: bfloat16 [4096, 256], P('ctx'), may hold values from -6 to 6
- conv_x: float32 [4, 5120], P(None, 'exp'), may hold values from -3 to 3
- conv_bc: float32 [4, 256], replicated, may hold values from -3 to 3
- log_decay: float32 [4096, 80], P('ctx', 'exp'), may hold values from -1 to 0
- skip_d: float32 [80], P('exp'), may hold values from 0.5 to 2
- norm_gain: float32 [5120], P('exp'), may hold values from 0.25 to 1.75
- routes: int32 [4096, 2], P('ctx'), may hold values from 0 to 31, all different within a row; in each aligned block of 128 rows (0 to 127, 128 to 255, ...) at most 12 rows name the same one
- route_gates: float32 [4096, 2], P('ctx'), may hold values from 0.2 to 1
- placement: int32 [32], replicated, may hold values from 0 to 31, each once
- gate_w: bfloat16 [32, 5120, 2048], P('ctx', None, 'exp'), may hold values from -0.078125 to 0.078125
- up_w: bfloat16 [32, 5120, 2048], P('ctx', None, 'exp'), may hold values from -0.078125 to 0.078125
- down_w: bfloat16 [32, 2048, 5120], P('ctx', 'exp'), may hold values from -0.125 to 0.125
Outputs:
- normed: bfloat16 [4096, 5120], P('ctx', 'exp')
- mixed: bfloat16 [4096, 5120], P('ctx', 'exp')
The draws below stay inside these ranges and needn't reach their ends.
Inputs may be any that keep to these rules, and one draw needn't show every extreme that they name: `routes`: in every aligned block of 128 tokens no expert is named by more than 12 choices, a bound that some block reaches; a token's two experts differ. `placement`: each slot holds exactly one expert.
All inputs are finite; a program needn't handle non-finite values.
Results may differ from the reference program's by a relative error of at most 0.023.
Values may be sent and summed in bfloat16 or wider, within the bound.
No kernel may reach another device: no remote copies, remote signals or barrier semaphores. Data moves between devices by JAX's collectives and lax.ppermute only.
A program may use at most 128 MiB of HBM per device.

```python
import math
import jax
import jax.numpy as jnp
import numpy as np
from jax import lax

HEADS = 80
HEAD_DIM = 64
STATE = 128
CONV = 4
FF = 2048
TOK_CTX = 128
D = 5120
SEQUENCE_TOKENS = 4096
EXPERTS = 32
CAP = 12
N_CTX = 32
N_EXP = 16


def draw_log_decay(key, part):
    key = jax.random.fold_in(key, 7)
    key_rate, key_scale, key_spot, key_loss = jax.random.split(key, 4)
    lowest = 0.02 / SEQUENCE_TOKENS
    highest = 1.0 / 30.0
    routing_rates = jnp.exp(jax.random.uniform(key_rate, (HEADS,), jnp.float32, jnp.log(lowest), jnp.log(highest)))
    expert_scales = jax.random.uniform(key_scale, (SEQUENCE_TOKENS, HEADS), jnp.float32, 0.5, 2.0)
    slot_positions = jax.random.randint(key_spot, (6,), 0, SEQUENCE_TOKENS)
    packed_token_rows = jnp.any(jnp.arange(SEQUENCE_TOKENS)[:, None] == slot_positions[None, :], axis=1)
    auxiliary_losses = jax.random.uniform(key_loss, (SEQUENCE_TOKENS, HEADS), jnp.float32, 0.2, 0.5)
    value_entries = -routing_rates[None, :] * expert_scales + jnp.where(packed_token_rows[:, None], jnp.log(1.0 - auxiliary_losses), 0.0)
    return value_entries.astype(jnp.float32)


def level_of(key, extent, cuts, smallest, top_value):
    def one(position, blocks):
        draws = jax.random.uniform(jax.random.fold_in(jax.random.fold_in(key, 6), position), (blocks,), jnp.float32, smallest / len(cuts), top_value / len(cuts))
        return jnp.repeat(jnp.exp(draws), extent[position] // blocks).reshape((-1,) + (1,) * (len(extent) - position - 1))

    factor_of = one(*cuts[0])
    for cut in cuts[1:]:
        factor_of = factor_of * one(*cut)
    return factor_of


def deal_out(key, own, number, rows, count, top, reach, lean):
    sequence = jax.random.permutation(key, count)
    heavy_load, ordinary = portions_of(count, rows * top, reach, lean, True), portions_of(count, rows * top, reach, lean, False)
    places = jnp.arange(count)

    def named(lengths, rotation):
        used = int((lengths > 0).sum())
        fixed = max(1, used // 4)
        shifted = fixed + (places - fixed + rotation * (used - fixed)) % max(1, count - fixed)
        return jnp.zeros((count,), jnp.int32).at[sequence[jnp.where(places < fixed, places, shifted)]].set(jnp.asarray(lengths, jnp.int32))

    lengths = jnp.where(number % 4 == 0, named(heavy_load, number // 4), named(ordinary, number - number // 4 - 1))
    mixed = jax.random.permutation(jax.random.fold_in(own, 3), count)
    donor, sink = mixed[0:count // 2 * 2:2], mixed[1:count // 2 * 2:2]
    room = jnp.minimum(lengths[donor] - 1, reach - lengths[sink]) // 2
    room = jnp.where((donor == sequence[0]) | (sink == sequence[0]) | (lengths[sink] == 0), 0, jnp.maximum(room, 0))
    shifted = jax.random.randint(jax.random.fold_in(own, 4), (count // 2,), 0, 1 << 20) % (room + 1)
    lengths = lengths.at[donor].add(-shifted).at[sink].add(shifted)
    items = jnp.searchsorted(jnp.cumsum(lengths), jnp.arange(rows * top), side="right").astype(jnp.int32)
    grid = items.reshape(top, rows).T
    grid = grid[jax.random.permutation(jax.random.fold_in(own, 1), rows)]
    rotation = jax.random.randint(jax.random.fold_in(own, 2), (rows, 1), 0, top)
    return jnp.take_along_axis(grid, (jnp.arange(top)[None, :] + rotation) % top, axis=1)


def portions_of(amount, total, reach, slope, full):
    weights = [(1 << 20) // math.isqrt(rank ** slope) + 1 for rank in range(1, amount + 1)]
    largest = reach if full else min(reach, max(-(-total // amount), total * weights[0] // sum(weights)))
    least = 1 if total - largest >= amount - 1 else 0
    given, rest = [largest] + [least] * (amount - 1), total - largest - least * (amount - 1)
    while rest > 0:
        candidates = [i for i in range(1, amount) if given[i] < largest] or [i for i in range(1, amount) if given[i] < reach]
        whole, left = sum([weights[i] for i in candidates]), rest
        for i in candidates:
            more = min(reach - given[i], max(1, left * weights[i] // whole), rest)
            given[i] = given[i] + more
            rest = rest - more
    return np.array(given)


def bell_draw(key, shape, deviation, most, cuts=(), held_as=jnp.bfloat16):
    loudness = level_of(key, shape, cuts, -0.22, 0.18) if cuts else 1.0
    array = jax.random.normal(key, shape, jnp.float32) * deviation * loudness
    return jnp.minimum(jnp.maximum(array, -most), most).astype(held_as)


def setup_inputs(seed: int = 0) -> dict:
    key_list = jax.random.split(jax.random.key(seed), 15)
    seq_x = bell_draw(key_list[0], (SEQUENCE_TOKENS, D), 1.0, 6.0, ((0, 32), (1, 16)))
    z_gate = bell_draw(key_list[1], (SEQUENCE_TOKENS, D), 1.0, 6.0, ((0, 32), (1, 16)))
    bc_in = bell_draw(key_list[2], (SEQUENCE_TOKENS, 2 * STATE), 1.0, 6.0, ((0, 32),))
    conv_x = bell_draw(key_list[3], (CONV, D), 0.6, 3.0, ((1, 16),), jnp.float32)
    conv_bc = bell_draw(key_list[4], (CONV, 2 * STATE), 0.6, 3.0, (), jnp.float32)
    log_decay = draw_log_decay(jax.random.fold_in(key_list[14], 71), 0)
    skip_d = jnp.clip(0.5 + 1.5 * jax.random.uniform(key_list[6], (HEADS,), jnp.float32) ** level_of(key_list[6], (HEADS,), ((0, 16),), -0.2, 0.2), 0.5, 2.0)
    norm_gain = jnp.clip(1.0 + 0.15 * jax.random.normal(key_list[7], (D,), jnp.float32), 0.25, 1.75)
    routes_keys = jax.random.split(jax.random.fold_in(key_list[8], 1), SEQUENCE_TOKENS // TOK_CTX)
    routes_turns = jax.random.permutation(jax.random.fold_in(key_list[8], 3), SEQUENCE_TOKENS // TOK_CTX)
    routes = jax.vmap(lambda own, number: deal_out(jax.random.fold_in(key_list[8], 2), own, number, TOK_CTX, EXPERTS, 2, CAP, 1))(routes_keys, routes_turns).reshape((SEQUENCE_TOKENS, 2))
    route_gates = jnp.clip(0.2 + 0.8 * jax.random.uniform(key_list[9], (SEQUENCE_TOKENS, 2), jnp.float32) ** level_of(key_list[9], (SEQUENCE_TOKENS, 2), ((0, 32),), -0.2, 0.2), 0.2, 1.0)
    placement = jax.random.permutation(key_list[10], EXPERTS).astype(jnp.int32)
    gate_w = bell_draw(key_list[11], (EXPERTS, D, FF), D ** -0.5, 0.078125, ((0, 32), (2, 16)))
    up_w = bell_draw(key_list[12], (EXPERTS, D, FF), D ** -0.5, 0.078125, ((0, 32), (2, 16)))
    down_w = bell_draw(key_list[13], (EXPERTS, FF, D), FF ** -0.5, 0.125, ((0, 32), (1, 16)))
    return dict(seq_x=seq_x, z_gate=z_gate, bc_in=bc_in, conv_x=conv_x, conv_bc=conv_bc, log_decay=log_decay, skip_d=skip_d, norm_gain=norm_gain, routes=routes, route_gates=route_gates, placement=placement, gate_w=gate_w, up_w=up_w, down_w=down_w)


def causal_conv(value_entries, kernel):
    width = kernel.shape[0]
    length = value_entries.shape[0]
    padded = jnp.concatenate([jnp.zeros((width - 1, value_entries.shape[1]), jnp.float32), value_entries], axis=0)
    total = jnp.zeros((length, value_entries.shape[1]), jnp.float32)
    for offset in range(width):
        total = total + kernel[offset][None, :] * padded[offset:offset + length]
    return total

def block_layout(route_rows):
    onehot = (route_rows[:, None] == jnp.arange(EXPERTS, dtype=jnp.int32)[None, :]).astype(jnp.int32)
    ranks = lax.optimization_barrier(jnp.sum(jnp.cumsum(onehot, axis=0) * onehot, axis=1)) - 1
    owners = lax.optimization_barrier(jnp.sum(onehot * placement_table[0][None, :], axis=1))
    return owners * CAP + ranks
placement_table = []

def reference(seq_x, z_gate, bc_in, conv_x, conv_bc, log_decay, skip_d, norm_gain, routes, route_gates, placement, gate_w, up_w, down_w):
    mixed_x = jax.nn.silu(causal_conv(seq_x.astype(jnp.float32), conv_x))
    mixed_bc = jax.nn.silu(causal_conv(bc_in.astype(jnp.float32), conv_bc))
    in_keys = mixed_bc[:, :STATE]
    out_keys = mixed_bc[:, STATE:]
    head_x = mixed_x.reshape(SEQUENCE_TOKENS, HEADS, HEAD_DIM)
    decays = jnp.exp(log_decay)

    def advance(state, inputs):
        row_x, row_in, row_out, row_decay = inputs
        state = row_decay[:, None, None] * state + row_x[:, :, None] * row_in[None, None, :]
        return (state, lax.optimization_barrier(jnp.sum(state * row_out[None, None, :], axis=-1)))
    start_state = jnp.zeros((HEADS, HEAD_DIM, STATE), jnp.float32)
    _, outputs = lax.scan(advance, start_state, (head_x, in_keys, out_keys, decays))
    outputs = outputs + skip_d[None, :, None] * head_x
    gated = outputs * jax.nn.silu(z_gate.astype(jnp.float32).reshape(SEQUENCE_TOKENS, HEADS, HEAD_DIM))
    expert_scales = lax.rsqrt(lax.optimization_barrier(jnp.mean(gated * gated, axis=-1, keepdims=True)) + 1e-05)
    normed = (gated * expert_scales * norm_gain.reshape(HEADS, HEAD_DIM)).reshape(SEQUENCE_TOKENS, D).astype(jnp.bfloat16)
    onehot_all = (routes.reshape(N_CTX, TOK_CTX * 2)[:, :, None] == jnp.arange(EXPERTS, dtype=jnp.int32)[None, None, :]).astype(jnp.int32)
    ranks = lax.optimization_barrier(jnp.sum(jnp.cumsum(onehot_all, axis=1) * onehot_all, axis=2)) - 1
    owners = lax.optimization_barrier(jnp.sum(onehot_all * placement[None, None, :], axis=2))
    positions = (owners * CAP + ranks).astype(jnp.int32)
    holders = (jnp.arange(TOK_CTX * 2, dtype=jnp.int32) // 2).astype(jnp.int32)

    def fill(pos_row):
        return jnp.full((EXPERTS * CAP,), TOK_CTX, jnp.int32).at[pos_row].set(holders)
    slot_token = jax.vmap(fill)(positions)
    shards = normed.reshape(N_CTX, TOK_CTX, D)
    padded = jnp.concatenate([shards, jnp.zeros((N_CTX, 1, D), jnp.bfloat16)], axis=1)
    buffers = jax.vmap(lambda rows_of, index_of: rows_of[index_of])(padded, slot_token)
    buffers = buffers.reshape(N_CTX, EXPERTS, CAP, D)
    group = FF // N_EXP

    def expert(slot):
        rows = buffers[:, slot].reshape(N_CTX * CAP, D).astype(jnp.float32)
        gate_part = gate_w[slot].astype(jnp.float32).reshape(D, N_EXP, group)
        up_part = up_w[slot].astype(jnp.float32).reshape(D, N_EXP, group)
        down_part = down_w[slot].astype(jnp.float32).reshape(N_EXP, group, D)
        gates = jnp.einsum('rd,dgf->rgf', rows, gate_part)
        ups = jnp.einsum('rd,dgf->rgf', rows, up_part)
        hidden = lax.optimization_barrier((jax.nn.silu(gates) * ups).astype(jnp.bfloat16)).astype(jnp.float32)
        parts = jnp.einsum('rgf,gfd->rgd', hidden, down_part)
        parts = lax.optimization_barrier(parts.astype(jnp.bfloat16)).astype(jnp.float32)
        return lax.optimization_barrier(jnp.sum(parts, axis=1)).reshape(N_CTX, CAP, D)
    results = lax.map(expert, jnp.arange(EXPERTS, dtype=jnp.int32))
    returned = jnp.transpose(results, (1, 0, 2, 3)).reshape(N_CTX, EXPERTS * CAP, D)
    picked = jax.vmap(lambda table, index_of: table[index_of])(returned, positions)
    weighted = picked.reshape(N_CTX, TOK_CTX, 2, D) * route_gates.reshape(N_CTX, TOK_CTX, 2, 1)
    mixed = lax.optimization_barrier(jnp.sum(weighted, axis=2)).reshape(SEQUENCE_TOKENS, D).astype(jnp.bfloat16)
    return (normed, mixed)
```

```python
import jax
import jax.numpy as jnp
from jax import lax
from jax.experimental import pallas as pl
from jax.experimental.pallas import tpu as pltpu
from jax.sharding import Mesh
from jax.sharding import PartitionSpec as P

HEAD_DIM = 64
STATE = 128
CONV = 4
CTX = ("zh", "zl", "c")
EXP = ("x", "y")
NEAR = ("zl", "c")
LANES = 128
HALF = 6
GROUPS = 5
PIECE = 32

BF = jnp.bfloat16
F32 = jnp.float32


def dot(a, b):
    return jnp.dot(a, b, preferred_element_type=F32)


def kernel_call(kernel, out_shape, count, scalars=1):
    specs = [pl.BlockSpec(memory_space=pltpu.SMEM)] * scalars
    specs += [pl.BlockSpec(memory_space=pltpu.VMEM)] * (count - scalars)
    return pl.pallas_call(
        kernel,
        out_shape=out_shape,
        in_specs=specs,
        out_specs=pl.BlockSpec(memory_space=pltpu.VMEM),
        compiler_params=pltpu.CompilerParams(vmem_limit_bytes=48 << 20),
    )


def gate_up_kernel(ix_ref, g_ref, w0_ref, w1_ref, w2_ref, w3_ref, out_ref):
    rows = 2 * 192
    wide = [jnp.concatenate([g_ref[y, :rows], g_ref[y, rows : 2 * rows]], axis=1) for y in range(4)]
    slim = []
    for y in range(4):
        packed = g_ref[y, 2 * rows :]
        slim.append(jnp.concatenate([packed[:, :64], packed[:, 64:]], axis=0))
    pairs = [jnp.concatenate([slim[0], slim[1]], axis=1), jnp.concatenate([slim[2], slim[3]], axis=1)]
    for s, w_ref in enumerate((w0_ref, w1_ref, w2_ref, w3_ref)):
        target = lax.rem(ix_ref[0] - s + 4, 4)

        def weight(start, size):
            return jnp.concatenate(
                [w_ref[start : start + size], w_ref[1280 + start : 1280 + start + size]], axis=1
            )

        total = dot(wide[0], weight(0, 256))
        for y in range(1, 4):
            total += dot(wide[y], weight(y * 320, 256))
        for p in range(2):
            low, high = weight(p * 640 + 256, 64), weight(p * 640 + 576, 64)
            total += dot(pairs[p], jnp.concatenate([low, high], axis=0))
        out_ref[target, :rows] = total[:, :LANES].astype(BF)
        out_ref[target, rows:] = total[:, LANES:].astype(BF)


def hidden_kernel(p_ref, out_ref):
    rows = p_ref.shape[1] // 2
    total = p_ref[0].astype(F32)
    for i in range(1, 4):
        total += p_ref[i].astype(F32)
    gate, up = total[:rows], total[rows:]
    out_ref[...] = (gate * jax.nn.sigmoid(gate) * up).astype(BF)


def down_kernel(ix_ref, h_ref, w0_ref, w1_ref, w2_ref, w3_ref, out_ref):
    rows = h_ref.shape[1]
    half = rows // 2
    hid = jnp.concatenate([h_ref[lax.rem(ix_ref[0] - s + 4, 4)] for s in range(4)], axis=1)
    blocks = []
    for b in range(5):
        weight = []
        for w_ref in (w0_ref, w1_ref, w2_ref, w3_ref):
            start = 2560 + b * 256
            weight.append(
                jnp.concatenate([w_ref[start : start + 128], w_ref[start + 128 : start + 256]], axis=1)
            )
        blocks.append(dot(hid, jnp.concatenate(weight, axis=0)))
    full = jnp.concatenate(blocks, axis=1)
    for y in range(4):
        own = full[:, y * 320 : (y + 1) * 320]
        out_ref[y, :rows] = own[:, :128].astype(BF)
        out_ref[y, rows : 2 * rows] = own[:, 128:256].astype(BF)
        last = own[:, 256:]
        out_ref[y, 2 * rows :] = jnp.concatenate([last[:half], last[half:]], axis=1).astype(BF)


def split_log(value):
    high = value.astype(BF)
    low = (value - high.astype(F32)).astype(BF)
    return high, low


def pack_state(state, logs):
    heads = logs.shape[0]
    tail = jnp.zeros((16, STATE), BF)
    high, low = split_log(logs)
    tail = tail.at[0, :heads].set(high).at[1, :heads].set(low)
    return jnp.concatenate([state.reshape(heads * HEAD_DIM, STATE).astype(BF), tail], axis=0)


def unpack_state(message, heads):
    rows = heads * HEAD_DIM
    states = message[:, :rows].astype(F32).reshape(-1, heads, HEAD_DIM, STATE)
    logs = message[:, rows, :heads].astype(F32) + message[:, rows + 1, :heads].astype(F32)
    return states, logs


def prefix(states, logs, end):
    count = logs.shape[0]
    places = jnp.arange(count)
    inside = (places[None, :] > places[:, None]) & (places[None, :] < end)
    gaps = jnp.sum(jnp.where(inside[:, :, None], logs[None], 0.0), axis=1)
    weights = jnp.where((places < end)[:, None], jnp.exp(gaps), 0.0)
    total = jnp.sum(weights[:, :, None, None] * states, axis=0)
    return total, jnp.sum(jnp.where((places < end)[:, None], logs, 0.0), axis=0)


def body(
    seq_x,
    z_gate,
    bc_in,
    conv_x,
    conv_bc,
    log_decay,
    skip_d,
    norm_gain,
    routes,
    route_gates,
    placement,
    gate_w,
    up_w,
    down_w,
):
    highest = lax.Precision.HIGHEST
    tokens, width = seq_x.shape
    heads = width // HEAD_DIM
    ix = lax.axis_index("x")

    edge = jnp.concatenate([seq_x[tokens - CONV + 1 :], bc_in[tokens - CONV + 1 :]], axis=1)
    rim = lax.ppermute(edge, CTX, [(i, i + 1) for i in range(31)])

    span = gate_w.shape[1] // 4
    gate_own, up_own = gate_w[0], up_w[0]
    down_own = down_w[0].reshape(LANES, 4 * span // LANES, LANES).transpose(1, 0, 2).reshape(4 * span, LANES)
    weights = []
    for s in range(4):
        start = lax.rem(ix + s, 4) * span
        piece = jnp.concatenate(
            [lax.dynamic_slice_in_dim(a, start, span, 0) for a in (gate_own, up_own, down_own)], axis=0
        )
        if s:
            piece = lax.ppermute(piece, "x", [(i, (i + s) % 4) for i in range(4)])
        weights.append(piece)

    experts = placement.shape[0]
    flat = routes.reshape(tokens * 2)
    onehot = (flat[:, None] == jnp.arange(experts, dtype=jnp.int32)[None, :]).astype(BF)
    places = jnp.arange(tokens * 2)
    tri = (places[:, None] > places[None, :]).astype(BF)
    before = dot(tri, onehot)
    hot = onehot.astype(F32)
    ranks = jnp.sum(before * hot, axis=1).astype(jnp.int32)
    owners = jnp.sum(hot * placement[None, :].astype(F32), axis=1).astype(jnp.int32)
    half = (ranks >= HALF).astype(jnp.int32)
    base = owners * PIECE + ranks - HALF * half
    half, base = half.reshape(tokens, 2), base.reshape(tokens, 2)
    columns = jnp.arange(experts * PIECE, dtype=jnp.int32)

    def table(values):
        planes = []
        for plane in range(4):
            if plane < 2:
                where, value = base + 2 * HALF * plane + HALF * half, values
            else:
                where, value = base + 4 * HALF, jnp.where(half == plane - 2, values, 0.0)
            hit = where[:, :, None] == columns[None, None, :]
            planes.append(jnp.sum(jnp.where(hit, value[:, :, None], 0.0), axis=1))
        return jnp.stack(planes)

    select = table(jnp.ones((tokens, 2), F32)).astype(BF)
    mixing = table(route_gates)

    long_x = jnp.concatenate([rim[:, :width], seq_x], axis=0).astype(F32)
    long_bc = jnp.concatenate([rim[:, width:], bc_in], axis=0).astype(F32)
    xs = jnp.zeros((tokens, width), F32)
    bcs = jnp.zeros((tokens, bc_in.shape[1]), F32)
    for offset in range(CONV):
        xs = xs + conv_x[offset][None, :] * long_x[offset : offset + tokens]
        bcs = bcs + conv_bc[offset][None, :] * long_bc[offset : offset + tokens]
    xs = jax.nn.silu(xs)
    bcs = jax.nn.silu(bcs)
    head_x = xs.reshape(tokens, heads, HEAD_DIM)
    in_keys, out_keys = bcs[:, :STATE], bcs[:, STATE:]
    steps = jnp.arange(tokens)
    lower = steps[:, None] >= steps[None, :]
    running = jnp.dot(lower.astype(F32), log_decay, precision=highest)
    tails = jnp.exp(running[-1:] - running)
    own_state = jnp.einsum("jh,jhp,jn->hpn", tails, head_x, in_keys, precision=highest)
    own_log = running[-1]

    near = lax.all_gather(pack_state(own_state, own_log), NEAR)
    near_states, near_logs = unpack_state(near, heads)
    count = near_logs.shape[0]
    near_carried, near_log = prefix(near_states, near_logs, lax.axis_index(NEAR))
    group_state, group_log = prefix(near_states, near_logs, count)
    far = lax.all_gather(pack_state(group_state, group_log), "zh")
    far_states, far_logs = unpack_state(far, heads)
    far_carried, _ = prefix(far_states, far_logs, lax.axis_index("zh"))
    carried = near_carried + jnp.exp(near_log)[:, None, None] * far_carried

    gaps = running[:, None, :] - running[None, :, :]
    weights_in = jnp.where(lower[:, :, None], jnp.exp(jnp.where(lower[:, :, None], gaps, 0.0)), 0.0)
    scores = jnp.einsum("in,jn->ij", out_keys, in_keys, precision=highest)
    inner = jnp.einsum("ij,ijh,jhp->ihp", scores, weights_in, head_x, precision=highest)
    outer = jnp.einsum("in,hpn->ihp", out_keys, carried, precision=highest) * jnp.exp(running)[..., None]
    outputs = inner + outer + skip_d[None, :, None] * head_x
    gated = outputs * jax.nn.silu(z_gate.astype(F32).reshape(tokens, heads, HEAD_DIM))
    scales = lax.rsqrt(jnp.mean(gated * gated, axis=-1, keepdims=True) + 1e-05)
    normed = (gated * scales * norm_gain.reshape(heads, HEAD_DIM)).reshape(tokens, width).astype(BF)

    blank = jnp.zeros((tokens, 64), BF)
    planes = jnp.stack(
        [
            normed[:, :128],
            normed[:, 128:256],
            jnp.concatenate([normed[:, 256:], blank], axis=1),
            jnp.concatenate([blank, normed[:, 256:]], axis=1),
        ]
    )
    outgoing = jnp.einsum("btj,btl->jl", select, planes, preferred_element_type=F32).astype(BF)
    arrived = lax.all_to_all(outgoing.reshape(experts, PIECE, LANES), CTX, 0, 0, tiled=True)
    rows = (
        arrived[:, : GROUPS * HALF]
        .reshape(experts, GROUPS, HALF, LANES)
        .transpose(1, 0, 2, 3)
        .reshape(GROUPS * experts * HALF, LANES)
    )
    wide = lax.all_gather(rows, "y")
    ixs = ix.reshape(1).astype(jnp.int32)
    count = 2 * experts * HALF
    parts = kernel_call(gate_up_kernel, jax.ShapeDtypeStruct((4, 2 * count, LANES), BF), 6)(
        ixs, wide, *weights
    )
    parts = lax.all_to_all(parts, "x", 0, 0, tiled=True)
    hidden = kernel_call(hidden_kernel, jax.ShapeDtypeStruct((count, LANES), BF), 1, 0)(parts)
    hiddens = lax.all_gather(hidden, "x")
    downs = kernel_call(down_kernel, jax.ShapeDtypeStruct((4, count * 5 // 2, LANES), BF), 6)(
        ixs, hiddens, *weights
    )
    downs = lax.all_to_all(downs, "y", 0, 0, tiled=True)
    result = jnp.sum(downs.astype(F32), axis=0).astype(BF)
    result = result.reshape(GROUPS, experts, HALF, LANES).transpose(1, 0, 2, 3)
    result = jnp.pad(result.reshape(experts, GROUPS * HALF, LANES), ((0, 0), (0, 2), (0, 0)))
    returned = lax.all_to_all(result, CTX, 0, 0, tiled=True).reshape(experts * PIECE, LANES)
    high, low = split_log(mixing)
    summed = jnp.einsum("btj,jl->btl", high, returned, preferred_element_type=F32) + jnp.einsum(
        "btj,jl->btl", low, returned, preferred_element_type=F32
    )
    mixed = jnp.concatenate([summed[0], summed[1], summed[2][:, :64] + summed[3][:, 64:]], axis=1)
    return (normed, mixed.astype(BF))


def solution(mesh):
    split = Mesh(mesh.devices.reshape(4, 4, 2, 4, 4), ("zh", "zl", "c", "x", "y"))
    placed = (
        P(CTX, EXP),
        P(CTX, EXP),
        P(CTX, None),
        P(None, EXP),
        P(),
        P(CTX, EXP),
        P(EXP),
        P(EXP),
        P(CTX, None),
        P(CTX, None),
        P(),
        P(CTX, None, EXP),
        P(CTX, None, EXP),
        P(CTX, EXP, None),
    )
    return jax.shard_map(
        body,
        mesh=split,
        in_specs=placed,
        out_specs=(P(CTX, EXP), P(CTX, EXP)),
        check_vma=False,
    )
```

```python
import jax
import jax.numpy as jnp
from jax import lax
from jax.experimental import pallas as pl
from jax.experimental.pallas import tpu as pltpu
from jax.sharding import Mesh
from jax.sharding import PartitionSpec as P

HEAD_DIM = 64
STATE = 128
CONV = 4
CTX = ("zh", "zl", "c")
EXP = ("x", "y")
NEAR = ("zl", "c")
LANES = 128
HALF = 6
GROUPS = 5
PIECE = 32

BF = jnp.bfloat16
F32 = jnp.float32


def dot(a, b):
    return jnp.dot(a, b, preferred_element_type=F32)


def kernel_call(kernel, outs, *operands, scalars=0, scratch=()):
    specs = [pl.BlockSpec(memory_space=pltpu.SMEM)] * scalars
    specs += [pl.BlockSpec(memory_space=pltpu.VMEM)] * (len(operands) - scalars)
    shapes = [jax.ShapeDtypeStruct(shape, kind) for shape, kind in outs]
    result = pl.pallas_call(
        kernel,
        out_shape=shapes,
        in_specs=specs,
        out_specs=[pl.BlockSpec(memory_space=pltpu.VMEM)] * len(outs),
        scratch_shapes=list(scratch),
        compiler_params=pltpu.CompilerParams(vmem_limit_bytes=48 << 20),
    )(*operands)
    return result[0] if len(outs) == 1 else result


def exact(a, b, dims=((1,), (0,))):
    return lax.dot_general(a, b, (dims, ((), ())), precision=lax.Precision.HIGHEST, preferred_element_type=F32)


def iota(shape, axis):
    return lax.broadcasted_iota(jnp.int32, shape, axis)


def silu(value):
    return value * jax.nn.sigmoid(value)


def turned(value):
    return value.astype(F32).T


def column(row):
    size = row.shape[1]
    hit = iota((size, size), 0) == iota((size, size), 1)
    return jnp.sum(jnp.where(hit, row.astype(F32), 0.0), axis=1, keepdims=True)


def edge_kernel(x_ref, bc_ref, out_ref):
    width, rows = x_ref.shape
    out_ref[:, :width] = turned(x_ref[...])[rows - 16 :].astype(BF)
    out_ref[:, width:384] = jnp.zeros((16, 384 - width), BF)
    out_ref[:, 384:] = bc_ref[rows - 16 :]


def route_kernel(routes_ref, row_ref, select_ref, pick_ref, half_ref):
    tokens = routes_ref.shape[1]
    experts = row_ref.shape[1]
    slots = experts * PIECE
    hot = [
        (column(routes_ref[k : k + 1]) == iota((tokens, experts), 1).astype(F32)).astype(F32)
        for k in range(2)
    ]
    earlier = (iota((tokens, tokens), 0) > iota((tokens, tokens), 1)).astype(BF)
    before = dot(earlier, (hot[0] + hot[1]).astype(BF))
    for k in range(2):
        rank = jnp.sum(hot[k] * before, axis=1, keepdims=True).astype(jnp.int32)
        owner = jnp.sum(hot[k] * row_ref[...].astype(F32), axis=1, keepdims=True).astype(jnp.int32)
        half = (rank >= HALF).astype(jnp.int32)
        base = owner * PIECE + rank - HALF * half
        half_ref[:, k : k + 1] = half.astype(F32)
        places = iota((tokens, slots), 1)
        for plane, where in enumerate((base + HALF * half, base + HALF * (half + 2), base + 4 * HALF)):
            start = (plane * 2 + k) * tokens
            pick_ref[start : start + tokens] = (places == where).astype(F32).astype(BF)
    hot = [(routes_ref[k : k + 1] == iota((experts, tokens), 0)).astype(F32) for k in range(2)]
    later = (iota((tokens, tokens), 0) < iota((tokens, tokens), 1)).astype(BF)
    before = dot((hot[0] + hot[1]).astype(BF), later)
    places = iota((slots, tokens), 0)
    planes = [jnp.zeros((slots, tokens), F32)] * 4
    owned = column(row_ref[...])
    for k in range(2):
        rank = jnp.sum(hot[k] * before, axis=0, keepdims=True).astype(jnp.int32)
        owner = jnp.sum(hot[k] * owned, axis=0, keepdims=True).astype(jnp.int32)
        half = (rank >= HALF).astype(jnp.int32)
        base = owner * PIECE + rank - HALF * half
        last = base + 4 * HALF
        wheres = (
            base + HALF * half,
            base + HALF * (half + 2),
            jnp.where(half == 0, last, -1),
            jnp.where(half == 1, last, -1),
        )
        planes = [p + (places == w).astype(F32) for p, w in zip(planes, wheres)]
    for plane in range(4):
        select_ref[:, plane * tokens : (plane + 1) * tokens] = planes[plane].astype(BF)


def spread(columns, heads):
    rows = columns.shape[0]
    return jnp.concatenate(
        [jnp.broadcast_to(columns[:, h : h + 1], (rows, HEAD_DIM)) for h in range(heads)], axis=1
    )


def write_logs(ref, start, logs):
    high = logs.astype(BF).astype(F32)
    places = iota((16, STATE), 0)
    tail = jnp.where(places == 0, high, jnp.where(places == 1, logs - high, 0.0))
    ref[start : start + 16] = tail.astype(BF)


def read_logs(tail):
    tail = tail.astype(F32)
    return tail[0:1] + tail[1:2]


def state_kernel(x_ref, bc_ref, rim_ref, cx_ref, cbc_ref, decay_ref, xs_ref, bcs_ref, run_ref, turn_ref, msg_ref, scratch):
    width, tokens = x_ref.shape
    heads = width // HEAD_DIM

    def conv(rim, value, taps):
        long = jnp.concatenate([rim.astype(F32), value], axis=0)
        total = taps[CONV - 1 : CONV] * long[16:]
        for back in range(1, CONV):
            total += taps[CONV - 1 - back : CONV - back] * pltpu.roll(long, back, 0)[16:]
        return silu(total)

    parts = []
    for start in range(0, width, LANES):
        stop = min(start + LANES, width)
        parts.append(conv(rim_ref[:, start:stop], turned(x_ref[start:stop]), cx_ref[:, start:stop]))
    xs = jnp.concatenate(parts, axis=1)
    bcs = conv(rim_ref[:, 384:], bc_ref[...].astype(F32), cbc_ref[...])
    lower = (iota((tokens, tokens), 0) >= iota((tokens, tokens), 1)).astype(F32)
    scratch[...] = jnp.zeros(scratch.shape, F32)
    scratch[:heads] = decay_ref[...]
    run = exact(lower, scratch[...], ((1,), (1,)))
    last = run[tokens - 1 : tokens]
    tails = jnp.exp(last - run)
    state = exact(xs * spread(tails, heads), bcs[:, :STATE], ((0,), (0,)))
    xs_ref[...] = xs
    bcs_ref[...] = bcs
    run_ref[...] = run
    turn_ref[...] = exact(scratch[...], lower, ((1,), (1,)))
    msg_ref[:width] = state.astype(BF)
    write_logs(msg_ref, width, last)


def inner_kernel(xs_ref, bcs_ref, run_ref, turn_ref, skip_ref, z_ref, y_ref, z_out_ref):
    tokens, width = xs_ref.shape
    lower = iota((tokens, tokens), 0) >= iota((tokens, tokens), 1)
    scores = exact(bcs_ref[:, STATE:], bcs_ref[:, :STATE], ((1,), (1,)))
    outs = []
    for h in range(width // HEAD_DIM):
        gaps = run_ref[:, h : h + 1] - turn_ref[h : h + 1]
        weight = jnp.where(lower, jnp.exp(jnp.where(lower, gaps, 0.0)), 0.0) * scores
        x = xs_ref[:, h * HEAD_DIM : (h + 1) * HEAD_DIM]
        outs.append(exact(weight, x) + skip_ref[h] * x)
    y_ref[...] = jnp.concatenate(outs, axis=1)
    z_out_ref[...] = silu(turned(z_ref[...]))


def near_kernel(place_ref, near_ref, carried_ref, log_ref, msg_ref, scratch):
    count, rows, _ = near_ref.shape
    rows -= 16
    heads = rows // HEAD_DIM
    total = [jnp.zeros((HEAD_DIM, STATE), F32)] * heads
    kept = total
    log = jnp.zeros((1, STATE), F32)
    kept_log = log
    for j in range(count):
        own = place_ref[0] == j
        kept = [jnp.where(own, t, k) for t, k in zip(total, kept)]
        kept_log = jnp.where(own, log, kept_log)
        step = read_logs(near_ref[j, rows:])
        factor = jnp.exp(step)
        log = log + step
        total = [
            factor[:, h : h + 1] * total[h] + near_ref[j, h * HEAD_DIM : (h + 1) * HEAD_DIM].astype(F32)
            for h in range(heads)
        ]
    for h in range(heads):
        carried_ref[h * HEAD_DIM : (h + 1) * HEAD_DIM] = kept[h]
        scratch[h * HEAD_DIM : (h + 1) * HEAD_DIM] = total[h].astype(BF)
    log_ref[...] = jnp.broadcast_to(kept_log, log_ref.shape)
    part = rows // 2
    msg_ref[:part] = scratch[pl.ds(pl.multiple_of(place_ref[1] * part, 32), part)]
    write_logs(msg_ref, part, log)


def far_kernel(place_ref, far_ref, out_ref):
    part = out_ref.shape[0]
    units = part // 32
    lanes = iota((1, STATE), 1)
    total = [jnp.zeros((32, STATE), F32)] * units
    for g in range(far_ref.shape[0] - 1):
        factor = jnp.exp(read_logs(far_ref[g, part:]))
        earlier = g < place_ref[2]
        for u in range(units):
            head = (place_ref[1] * units + u) // 2
            one = jnp.sum(jnp.where(lanes == head, factor, 0.0), axis=1, keepdims=True)
            state = far_ref[g, u * 32 : (u + 1) * 32].astype(F32)
            total[u] = jnp.where(earlier, one * total[u] + state, total[u])
    for u in range(units):
        out_ref[u * 32 : (u + 1) * 32] = total[u].astype(BF)


def finish_kernel(
    place_ref, own_ref, other_ref, near_ref, log_ref, bcs_ref, run_ref, y_ref, z_ref, gain_ref, select_ref,
    normed_ref, out_ref, scratch,
):
    part = own_ref.shape[0]
    tokens, width = y_ref.shape
    heads = width // HEAD_DIM
    core = place_ref[1]
    scratch[pl.ds(pl.multiple_of(core * part, 32), part)] = own_ref[...]
    scratch[pl.ds(pl.multiple_of((1 - core) * part, 32), part)] = other_ref[...]
    factor = jnp.exp(log_ref[0:1])
    carried = jnp.concatenate(
        [
            near_ref[h * HEAD_DIM : (h + 1) * HEAD_DIM]
            + factor[:, h : h + 1] * scratch[h * HEAD_DIM : (h + 1) * HEAD_DIM].astype(F32)
            for h in range(heads)
        ],
        axis=0,
    )
    outer = exact(bcs_ref[:, STATE:], carried, ((1,), (1,))) * spread(jnp.exp(run_ref[...]), heads)
    gated = (y_ref[...] + outer) * z_ref[...]
    square = gated * gated
    scales = jnp.concatenate(
        [
            jnp.broadcast_to(
                lax.rsqrt(
                    jnp.mean(square[:, h * HEAD_DIM : (h + 1) * HEAD_DIM], axis=1, keepdims=True) + 1e-05
                ),
                (tokens, HEAD_DIM),
            )
            for h in range(heads)
        ],
        axis=1,
    )
    normed = (gated * scales * gain_ref[...]).astype(BF)
    normed_ref[...] = turned(normed).astype(BF)
    blank = jnp.zeros((tokens, 64), BF)
    planes = jnp.concatenate(
        [
            normed[:, :128],
            normed[:, 128:256],
            jnp.concatenate([normed[:, 256:], blank], axis=1),
            jnp.concatenate([blank, normed[:, 256:]], axis=1),
        ],
        axis=0,
    )
    out_ref[...] = dot(select_ref[...], planes).astype(BF)


def piece_kernel(block_ref, gate_ref, up_ref, down_ref, out_ref):
    span = gate_ref.shape[0]
    out_ref[:span] = gate_ref[...]
    out_ref[span : 2 * span] = up_ref[...]
    for b in range(span // LANES):
        start = 2 * span + b * LANES
        out_ref[start : start + LANES] = down_ref[:, b * LANES : (b + 1) * LANES]


def weight_piece(block, gate, up, down):
    span = gate.shape[0] // 4
    return pl.pallas_call(
        piece_kernel,
        out_shape=jax.ShapeDtypeStruct((3 * span, LANES), BF),
        grid_spec=pltpu.PrefetchScalarGridSpec(
            num_scalar_prefetch=1,
            grid=(1,),
            in_specs=[
                pl.BlockSpec((span, LANES), lambda i, b: (b[0], 0)),
                pl.BlockSpec((span, LANES), lambda i, b: (b[0], 0)),
                pl.BlockSpec((LANES, span), lambda i, b: (0, b[0])),
            ],
            out_specs=pl.BlockSpec((3 * span, LANES), lambda i, b: (0, 0)),
        ),
        compiler_params=pltpu.CompilerParams(vmem_limit_bytes=32 << 20),
    )(block, gate, up, down)


def mix_kernel(pick_ref, rows_ref, gates_ref, half_ref, out_ref):
    tokens = gates_ref.shape[1]
    picked = dot(pick_ref[...], rows_ref[...])
    totals = [0.0, 0.0, 0.0]
    for k in range(2):
        gate = column(gates_ref[k : k + 1])
        for plane in range(3):
            start = (plane * 2 + k) * tokens
            one = picked[start : start + tokens]
            if plane == 2:
                one = jnp.where(half_ref[:, k : k + 1] > 0.5, one[:, 64:], one[:, :64])
            totals[plane] = totals[plane] + gate * one
    for plane in range(3):
        size = min(LANES, out_ref.shape[0] - plane * LANES)
        out_ref[plane * LANES : plane * LANES + size] = totals[plane].T.astype(BF)


def gate_up_kernel(ix_ref, g_ref, w0_ref, w1_ref, w2_ref, w3_ref, out_ref):
    rows = 2 * 192
    wide = [jnp.concatenate([g_ref[y, :rows], g_ref[y, rows : 2 * rows]], axis=1) for y in range(4)]
    slim = []
    for y in range(4):
        packed = g_ref[y, 2 * rows :]
        slim.append(jnp.concatenate([packed[:, :64], packed[:, 64:]], axis=0))
    pairs = [jnp.concatenate([slim[0], slim[1]], axis=1), jnp.concatenate([slim[2], slim[3]], axis=1)]
    for s, w_ref in enumerate((w0_ref, w1_ref, w2_ref, w3_ref)):
        target = lax.rem(ix_ref[0] - s + 4, 4)

        def weight(start, size):
            return jnp.concatenate(
                [w_ref[start : start + size], w_ref[1280 + start : 1280 + start + size]], axis=1
            )

        total = dot(wide[0], weight(0, 256))
        for y in range(1, 4):
            total += dot(wide[y], weight(y * 320, 256))
        for p in range(2):
            low, high = weight(p * 640 + 256, 64), weight(p * 640 + 576, 64)
            total += dot(pairs[p], jnp.concatenate([low, high], axis=0))
        out_ref[target, :rows] = total[:, :LANES].astype(BF)
        out_ref[target, rows:] = total[:, LANES:].astype(BF)


def hidden_kernel(p_ref, out_ref):
    rows = p_ref.shape[1] // 2
    total = p_ref[0].astype(F32)
    for i in range(1, 4):
        total += p_ref[i].astype(F32)
    gate, up = total[:rows], total[rows:]
    hidden = (silu(gate) * up).astype(BF)
    for i in range(4):
        out_ref[i] = hidden


def down_kernel(ix_ref, h_ref, w0_ref, w1_ref, w2_ref, w3_ref, out_ref):
    rows = h_ref.shape[1]
    half = rows // 2
    hid = jnp.concatenate([h_ref[lax.rem(ix_ref[0] - s + 4, 4)] for s in range(4)], axis=1)
    blocks = []
    for b in range(5):
        weight = []
        for w_ref in (w0_ref, w1_ref, w2_ref, w3_ref):
            start = 2560 + b * 256
            weight.append(
                jnp.concatenate([w_ref[start : start + 128], w_ref[start + 128 : start + 256]], axis=1)
            )
        blocks.append(dot(hid, jnp.concatenate(weight, axis=0)))
    full = jnp.concatenate(blocks, axis=1)
    for y in range(4):
        own = full[:, y * 320 : (y + 1) * 320]
        out_ref[y, :rows] = own[:, :128].astype(BF)
        out_ref[y, rows : 2 * rows] = own[:, 128:256].astype(BF)
        last = own[:, 256:]
        out_ref[y, 2 * rows :] = jnp.concatenate([last[:half], last[half:]], axis=1).astype(BF)


def body(
    seq_x,
    z_gate,
    bc_in,
    conv_x,
    conv_bc,
    log_decay,
    skip_d,
    norm_gain,
    routes,
    route_gates,
    placement,
    gate_w,
    up_w,
    down_w,
):
    tokens, width = seq_x.shape
    heads = width // HEAD_DIM
    experts = placement.shape[0]
    slots = experts * PIECE
    ix = lax.axis_index("x").astype(jnp.int32)
    place = jnp.stack([lax.axis_index(NEAR), lax.axis_index("c"), lax.axis_index("zh")]).astype(jnp.int32)

    edge = kernel_call(edge_kernel, [((16, 640), BF)], seq_x.T, bc_in)
    rim = lax.ppermute(edge, CTX, [(i, i + 1) for i in range(31)])
    select, pick, half = kernel_call(
        route_kernel,
        [((slots, 4 * tokens), BF), ((6 * tokens, slots), BF), ((tokens, 2), F32)],
        routes.T,
        placement.reshape(1, experts),
    )
    ixs = ix.reshape(1)
    pieces = {s: weight_piece(lax.rem(ixs + s, 4), gate_w[0], up_w[0], down_w[0]) for s in (1, 3, 2, 0)}
    swapped = {s: lax.ppermute(pieces[s], "x", [(i, (i + s) % 4) for i in range(4)]) for s in (1, 3, 2)}
    rim, select, pick, half, held = lax.optimization_barrier((rim, select, pick, half, pieces[1]))
    xs, bcs, run, turn, message = kernel_call(
        state_kernel,
        [
            ((tokens, width), F32),
            ((tokens, 2 * STATE), F32),
            ((tokens, STATE), F32),
            ((STATE, tokens), F32),
            ((width + 16, STATE), BF),
        ],
        seq_x.T,
        bc_in,
        rim,
        conv_x,
        conv_bc,
        log_decay.T,
        scratch=[pltpu.VMEM((STATE, tokens), F32)],
    )
    near = lax.all_gather(message, NEAR)
    near, swapped[1], swapped[3] = lax.optimization_barrier((near, swapped[1], swapped[3]))
    near_carried, near_log, group = kernel_call(
        near_kernel,
        [((width, STATE), F32), ((8, STATE), F32), ((width // 2 + 16, STATE), BF)],
        place,
        near,
        scalars=1,
        scratch=[pltpu.VMEM((width, STATE), BF)],
    )
    fars = lax.all_gather(group, "zh")
    turn, group = lax.optimization_barrier((turn, group))
    y_in, z_in = pl.pallas_call(
        inner_kernel,
        out_shape=[jax.ShapeDtypeStruct((tokens, width), F32)] * 2,
        in_specs=[pl.BlockSpec(memory_space=pltpu.VMEM)] * 4
        + [pl.BlockSpec(memory_space=pltpu.SMEM), pl.BlockSpec(memory_space=pltpu.VMEM)],
        out_specs=[pl.BlockSpec(memory_space=pltpu.VMEM)] * 2,
        compiler_params=pltpu.CompilerParams(vmem_limit_bytes=32 << 20),
    )(xs, bcs, run, turn, skip_d, z_gate.T)
    far = kernel_call(far_kernel, [((width // 2, STATE), BF)], place, fars, scalars=1)
    other = lax.ppermute(far, "c", [(0, 1), (1, 0)])
    normed, outgoing = kernel_call(
        finish_kernel,
        [((width, tokens), BF), ((slots, LANES), BF)],
        place,
        far,
        other,
        near_carried,
        near_log,
        bcs,
        run,
        y_in,
        z_in,
        norm_gain.reshape(1, width),
        select,
        scalars=1,
        scratch=[pltpu.VMEM((width, STATE), BF)],
    )
    arrived = lax.all_to_all(outgoing.reshape(experts, PIECE, LANES), CTX, 0, 0, tiled=True)
    rows = (
        arrived[:, : GROUPS * HALF]
        .reshape(experts, GROUPS, HALF, LANES)
        .transpose(1, 0, 2, 3)
        .reshape(GROUPS * experts * HALF, LANES)
    )
    wide = lax.all_gather(rows, "y")
    count = 2 * experts * HALF
    weights = [pieces[0], swapped[1], swapped[2], swapped[3]]
    parts = kernel_call(gate_up_kernel, [((4, 2 * count, LANES), BF)], ixs, wide, *weights, scalars=1)
    parts = lax.all_to_all(parts, "x", 0, 0, tiled=True)
    hidden = kernel_call(hidden_kernel, [((4, count, LANES), BF)], parts)
    hiddens = lax.all_to_all(hidden, "x", 0, 0, tiled=True)
    downs = kernel_call(down_kernel, [((4, count * 5 // 2, LANES), BF)], ixs, hiddens, *weights, scalars=1)
    downs = lax.all_to_all(downs, "y", 0, 0, tiled=True)
    result = jnp.sum(downs.astype(F32), axis=0).astype(BF)
    result = result.reshape(GROUPS, experts, HALF, LANES).transpose(1, 0, 2, 3)
    result = jnp.pad(result.reshape(experts, GROUPS * HALF, LANES), ((0, 0), (0, 2), (0, 0)))
    returned = lax.all_to_all(result, CTX, 0, 0, tiled=True).reshape(slots, LANES)
    mixed = kernel_call(mix_kernel, [((width, tokens), BF)], pick, returned, route_gates.T, half)
    return (normed.T, mixed.T)


def solution(mesh):
    split = Mesh(mesh.devices.reshape(4, 4, 2, 4, 4), ("zh", "zl", "c", "x", "y"))
    placed = (
        P(CTX, EXP),
        P(CTX, EXP),
        P(CTX, None),
        P(None, EXP),
        P(),
        P(CTX, EXP),
        P(EXP),
        P(EXP),
        P(CTX, None),
        P(CTX, None),
        P(),
        P(CTX, None, EXP),
        P(CTX, None, EXP),
        P(CTX, EXP, None),
    )
    return jax.shard_map(
        body,
        mesh=split,
        in_specs=placed,
        out_specs=(P(CTX, EXP), P(CTX, EXP)),
        check_vma=False,
    )
```

```python
import functools

import jax
import jax.numpy as jnp
from jax import lax
from jax.experimental import pallas as pl
from jax.experimental.pallas import tpu as pltpu
from jax.sharding import Mesh
from jax.sharding import PartitionSpec as P

HEAD_DIM = 64
STATE = 128
CONV = 4
CTX = ("zh", "zl", "c")
EXP = ("x", "y")
NEAR = ("zl", "c")
LANES = 128
HALF = 6
GROUPS = 5
PIECE = 32

BF = jnp.bfloat16
F32 = jnp.float32


def dot(a, b):
    return jnp.dot(a, b, preferred_element_type=F32)


def kernel_call(kernel, outs, *operands, scalars=0, scratch=()):
    specs = [pl.BlockSpec(memory_space=pltpu.SMEM)] * scalars
    specs += [pl.BlockSpec(memory_space=pltpu.VMEM)] * (len(operands) - scalars)
    shapes = [jax.ShapeDtypeStruct(shape, kind) for shape, kind in outs]
    result = pl.pallas_call(
        kernel,
        out_shape=shapes,
        in_specs=specs,
        out_specs=[pl.BlockSpec(memory_space=pltpu.VMEM)] * len(outs),
        scratch_shapes=list(scratch),
        compiler_params=pltpu.CompilerParams(vmem_limit_bytes=20 << 20),
    )(*operands)
    return result[0] if len(outs) == 1 else result


def exact(a, b, dims=((1,), (0,))):
    return lax.dot_general(a, b, (dims, ((), ())), precision=lax.Precision.HIGHEST, preferred_element_type=F32)


def iota(shape, axis):
    return lax.broadcasted_iota(jnp.int32, shape, axis)


def silu(value):
    return value * jax.nn.sigmoid(value)


def turned(value):
    return value.astype(F32).T


def column(row):
    size = row.shape[1]
    hit = iota((size, size), 0) == iota((size, size), 1)
    return jnp.sum(jnp.where(hit, row.astype(F32), 0.0), axis=1, keepdims=True)


def edge_kernel(x_ref, bc_ref, out_ref):
    width, rows = x_ref.shape
    out_ref[:, :width] = turned(x_ref[...])[rows - 16 :].astype(BF)
    out_ref[:, width:384] = jnp.zeros((16, 384 - width), BF)
    out_ref[:, 384:] = bc_ref[rows - 16 :]


def pick_kernel(routes_ref, row_ref, pick_ref, half_ref):
    tokens = routes_ref.shape[1]
    experts = row_ref.shape[1]
    slots = experts * PIECE
    hot = [
        (column(routes_ref[k : k + 1]) == iota((tokens, experts), 1).astype(F32)).astype(F32)
        for k in range(2)
    ]
    earlier = (iota((tokens, tokens), 0) > iota((tokens, tokens), 1)).astype(BF)
    before = dot(earlier, (hot[0] + hot[1]).astype(BF))
    for k in range(2):
        rank = jnp.sum(hot[k] * before, axis=1, keepdims=True).astype(jnp.int32)
        owner = jnp.sum(hot[k] * row_ref[...].astype(F32), axis=1, keepdims=True).astype(jnp.int32)
        half = (rank >= HALF).astype(jnp.int32)
        base = owner * PIECE + rank - HALF * half
        half_ref[:, k : k + 1] = half.astype(F32)
        places = iota((tokens, slots), 1)
        for plane, where in enumerate((base + HALF * half, base + HALF * (half + 2), base + 4 * HALF)):
            start = (plane * 2 + k) * tokens
            pick_ref[start : start + tokens] = (places == where).astype(F32).astype(BF)


def select_kernel(routes_ref, row_ref, select_ref):
    tokens = routes_ref.shape[1]
    experts = row_ref.shape[1]
    slots = experts * PIECE
    hot = [(routes_ref[k : k + 1] == iota((experts, tokens), 0)).astype(F32) for k in range(2)]
    later = (iota((tokens, tokens), 0) < iota((tokens, tokens), 1)).astype(BF)
    before = dot((hot[0] + hot[1]).astype(BF), later)
    places = iota((slots, tokens), 0)
    planes = [jnp.zeros((slots, tokens), F32)] * 4
    owned = column(row_ref[...])
    for k in range(2):
        rank = jnp.sum(hot[k] * before, axis=0, keepdims=True).astype(jnp.int32)
        owner = jnp.sum(hot[k] * owned, axis=0, keepdims=True).astype(jnp.int32)
        half = (rank >= HALF).astype(jnp.int32)
        base = owner * PIECE + rank - HALF * half
        last = base + 4 * HALF
        wheres = (
            base + HALF * half,
            base + HALF * (half + 2),
            jnp.where(half == 0, last, -1),
            jnp.where(half == 1, last, -1),
        )
        planes = [p + (places == w).astype(F32) for p, w in zip(planes, wheres)]
    for plane in range(4):
        select_ref[:, plane * tokens : (plane + 1) * tokens] = planes[plane].astype(BF)


def spread(columns, heads):
    rows = columns.shape[0]
    return jnp.concatenate(
        [jnp.broadcast_to(columns[:, h : h + 1], (rows, HEAD_DIM)) for h in range(heads)], axis=1
    )


def write_logs(ref, start, logs):
    high = logs.astype(BF).astype(F32)
    places = iota((16, STATE), 0)
    tail = jnp.where(places == 0, high, jnp.where(places == 1, logs - high, 0.0))
    ref[start : start + 16] = tail.astype(BF)


def read_logs(tail):
    tail = tail.astype(F32)
    return tail[0:1] + tail[1:2]


def state_kernel(x_ref, bc_ref, rim_ref, cx_ref, cbc_ref, decay_ref, xs_ref, bcs_ref, run_ref, turn_ref, msg_ref, scratch):
    width, tokens = x_ref.shape
    heads = width // HEAD_DIM

    def conv(rim, value, taps):
        long = jnp.concatenate([rim.astype(F32), value], axis=0)
        total = taps[CONV - 1 : CONV] * long[16:]
        for back in range(1, CONV):
            total += taps[CONV - 1 - back : CONV - back] * pltpu.roll(long, back, 0)[16:]
        return silu(total)

    parts = []
    for start in range(0, width, LANES):
        stop = min(start + LANES, width)
        parts.append(conv(rim_ref[:, start:stop], turned(x_ref[start:stop]), cx_ref[:, start:stop]))
    xs = jnp.concatenate(parts, axis=1)
    bcs = conv(rim_ref[:, 384:], bc_ref[...].astype(F32), cbc_ref[...])
    lower = (iota((tokens, tokens), 0) >= iota((tokens, tokens), 1)).astype(F32)
    scratch[...] = jnp.zeros(scratch.shape, F32)
    scratch[:heads] = decay_ref[...]
    run = exact(lower, scratch[...], ((1,), (1,)))
    last = run[tokens - 1 : tokens]
    tails = jnp.exp(last - run)
    state = exact(xs * spread(tails, heads), bcs[:, :STATE], ((0,), (0,)))
    xs_ref[...] = xs
    bcs_ref[...] = bcs
    run_ref[...] = run
    turn_ref[...] = exact(scratch[...], lower, ((1,), (1,)))
    msg_ref[:width] = state.astype(BF)
    write_logs(msg_ref, width, last)


def inner_kernel(xs_ref, bcs_ref, run_ref, turn_ref, skip_ref, z_ref, y_ref, z_out_ref):
    tokens, width = xs_ref.shape
    lower = iota((tokens, tokens), 0) >= iota((tokens, tokens), 1)
    scores = exact(bcs_ref[:, STATE:], bcs_ref[:, :STATE], ((1,), (1,)))
    outs = []
    for h in range(width // HEAD_DIM):
        gaps = run_ref[:, h : h + 1] - turn_ref[h : h + 1]
        weight = jnp.where(lower, jnp.exp(jnp.where(lower, gaps, 0.0)), 0.0) * scores
        x = xs_ref[:, h * HEAD_DIM : (h + 1) * HEAD_DIM]
        outs.append(exact(weight, x) + skip_ref[h] * x)
    y_ref[...] = jnp.concatenate(outs, axis=1)
    z_out_ref[...] = silu(turned(z_ref[...]))


def near_kernel(place_ref, near_ref, carried_ref, log_ref, msg_ref, scratch):
    count, rows, _ = near_ref.shape
    rows -= 16
    heads = rows // HEAD_DIM
    total = [jnp.zeros((HEAD_DIM, STATE), F32)] * heads
    kept = total
    log = jnp.zeros((1, STATE), F32)
    kept_log = log
    for j in range(count):
        own = place_ref[0] == j
        kept = [jnp.where(own, t, k) for t, k in zip(total, kept)]
        kept_log = jnp.where(own, log, kept_log)
        step = read_logs(near_ref[j, rows:])
        factor = jnp.exp(step)
        log = log + step
        total = [
            factor[:, h : h + 1] * total[h] + near_ref[j, h * HEAD_DIM : (h + 1) * HEAD_DIM].astype(F32)
            for h in range(heads)
        ]
    for h in range(heads):
        carried_ref[h * HEAD_DIM : (h + 1) * HEAD_DIM] = kept[h]
        scratch[h * HEAD_DIM : (h + 1) * HEAD_DIM] = total[h].astype(BF)
    log_ref[...] = jnp.broadcast_to(kept_log, log_ref.shape)
    part = rows // 2
    msg_ref[:part] = scratch[pl.ds(pl.multiple_of(place_ref[1] * part, 32), part)]
    write_logs(msg_ref, part, log)


def far_kernel(place_ref, far_ref, out_ref):
    part = out_ref.shape[0]
    units = part // 32
    lanes = iota((1, STATE), 1)
    total = [jnp.zeros((32, STATE), F32)] * units
    for g in range(far_ref.shape[0] - 1):
        factor = jnp.exp(read_logs(far_ref[g, part:]))
        earlier = g < place_ref[2]
        for u in range(units):
            head = (place_ref[1] * units + u) // 2
            one = jnp.sum(jnp.where(lanes == head, factor, 0.0), axis=1, keepdims=True)
            state = far_ref[g, u * 32 : (u + 1) * 32].astype(F32)
            total[u] = jnp.where(earlier, one * total[u] + state, total[u])
    for u in range(units):
        out_ref[u * 32 : (u + 1) * 32] = total[u].astype(BF)


def finish_kernel(
    place_ref, own_ref, other_ref, near_ref, log_ref, bcs_ref, run_ref, y_ref, z_ref, gain_ref, select_ref,
    normed_ref, out_ref, scratch,
):
    part = own_ref.shape[0]
    tokens, width = y_ref.shape
    heads = width // HEAD_DIM
    core = place_ref[1]
    scratch[pl.ds(pl.multiple_of(core * part, 32), part)] = own_ref[...]
    scratch[pl.ds(pl.multiple_of((1 - core) * part, 32), part)] = other_ref[...]
    factor = jnp.exp(log_ref[0:1])
    carried = jnp.concatenate(
        [
            near_ref[h * HEAD_DIM : (h + 1) * HEAD_DIM]
            + factor[:, h : h + 1] * scratch[h * HEAD_DIM : (h + 1) * HEAD_DIM].astype(F32)
            for h in range(heads)
        ],
        axis=0,
    )
    outer = exact(bcs_ref[:, STATE:], carried, ((1,), (1,))) * spread(jnp.exp(run_ref[...]), heads)
    gated = (y_ref[...] + outer) * z_ref[...]
    square = gated * gated
    scales = jnp.concatenate(
        [
            jnp.broadcast_to(
                lax.rsqrt(
                    jnp.mean(square[:, h * HEAD_DIM : (h + 1) * HEAD_DIM], axis=1, keepdims=True) + 1e-05
                ),
                (tokens, HEAD_DIM),
            )
            for h in range(heads)
        ],
        axis=1,
    )
    normed = (gated * scales * gain_ref[...]).astype(BF)
    normed_ref[...] = turned(normed).astype(BF)
    blank = jnp.zeros((tokens, 64), BF)
    planes = jnp.concatenate(
        [
            normed[:, :128],
            normed[:, 128:256],
            jnp.concatenate([normed[:, 256:], blank], axis=1),
            jnp.concatenate([blank, normed[:, 256:]], axis=1),
        ],
        axis=0,
    )
    out_ref[...] = dot(select_ref[...], planes).astype(BF)


def piece_kernel(steps, ix_ref, gate_ref, up_ref, down_ref, *rest):
    outs, (held, in_sems, out_sems) = rest[: len(steps)], rest[len(steps) :]
    span = gate_ref.shape[0] // 4
    arrivals = []
    for i, step in enumerate(steps):
        block = pl.multiple_of(lax.rem(ix_ref[0] + step, 4) * span, span)
        pairs = [
            (gate_ref.at[pl.ds(block, span)], held.at[i, pl.ds(0, span)]),
            (up_ref.at[pl.ds(block, span)], held.at[i, pl.ds(span, span)]),
        ]
        for b in range(span // LANES):
            pairs.append(
                (
                    down_ref.at[:, pl.ds(pl.multiple_of(block + b * LANES, LANES), LANES)],
                    held.at[i, pl.ds(2 * span + b * LANES, LANES)],
                )
            )
        arrivals.append(
            [pltpu.make_async_copy(p, q, in_sems.at[i, n]) for n, (p, q) in enumerate(pairs)]
        )
    for copies in arrivals:
        for copy in copies:
            copy.start()
    departures = []
    for i, copies in enumerate(arrivals):
        for copy in copies:
            copy.wait()
        departures.append(pltpu.make_async_copy(held.at[i], outs[i], out_sems.at[i]))
        departures[i].start()
    for copy in departures:
        copy.wait()


def weight_pieces(steps, ix, gate, up, down):
    span = gate.shape[0] // 4
    count = len(steps)
    whole = pl.BlockSpec(memory_space=pltpu.HBM)
    return pl.pallas_call(
        functools.partial(piece_kernel, steps),
        out_shape=[jax.ShapeDtypeStruct((3 * span, LANES), BF)] * count,
        in_specs=[pl.BlockSpec(memory_space=pltpu.SMEM), whole, whole, whole],
        out_specs=[whole] * count,
        scratch_shapes=[
            pltpu.VMEM((count, 3 * span, LANES), BF),
            pltpu.SemaphoreType.DMA((count, 2 + span // LANES)),
            pltpu.SemaphoreType.DMA((count,)),
        ],
        compiler_params=pltpu.CompilerParams(vmem_limit_bytes=60 << 20),
    )(ix, gate, up, down)


def mix_kernel(pick_ref, rows_ref, gates_ref, half_ref, out_ref):
    tokens = gates_ref.shape[1]
    picked = dot(pick_ref[...], rows_ref[...])
    totals = [0.0, 0.0, 0.0]
    for k in range(2):
        gate = column(gates_ref[k : k + 1])
        for plane in range(3):
            start = (plane * 2 + k) * tokens
            one = picked[start : start + tokens]
            if plane == 2:
                one = jnp.where(half_ref[:, k : k + 1] > 0.5, one[:, 64:], one[:, :64])
            totals[plane] = totals[plane] + gate * one
    for plane in range(3):
        size = min(LANES, out_ref.shape[0] - plane * LANES)
        out_ref[plane * LANES : plane * LANES + size] = totals[plane].T.astype(BF)


def gate_up_kernel(ix_ref, g_ref, w0_ref, w1_ref, w2_ref, w3_ref, out_ref):
    rows = 2 * 192
    wide = [jnp.concatenate([g_ref[y, :rows], g_ref[y, rows : 2 * rows]], axis=1) for y in range(4)]
    slim = []
    for y in range(4):
        packed = g_ref[y, 2 * rows :]
        slim.append(jnp.concatenate([packed[:, :64], packed[:, 64:]], axis=0))
    pairs = [jnp.concatenate([slim[0], slim[1]], axis=1), jnp.concatenate([slim[2], slim[3]], axis=1)]
    for s, w_ref in enumerate((w0_ref, w1_ref, w2_ref, w3_ref)):
        target = lax.rem(ix_ref[0] - s + 4, 4)

        def weight(start, size):
            return jnp.concatenate(
                [w_ref[start : start + size], w_ref[1280 + start : 1280 + start + size]], axis=1
            )

        total = dot(wide[0], weight(0, 256))
        for y in range(1, 4):
            total += dot(wide[y], weight(y * 320, 256))
        for p in range(2):
            low, high = weight(p * 640 + 256, 64), weight(p * 640 + 576, 64)
            total += dot(pairs[p], jnp.concatenate([low, high], axis=0))
        out_ref[target, :rows] = total[:, :LANES].astype(BF)
        out_ref[target, rows:] = total[:, LANES:].astype(BF)


def hidden_kernel(p_ref, out_ref):
    rows = p_ref.shape[1] // 2
    total = p_ref[0].astype(F32)
    for i in range(1, 4):
        total += p_ref[i].astype(F32)
    gate, up = total[:rows], total[rows:]
    hidden = (silu(gate) * up).astype(BF)
    for i in range(4):
        out_ref[i] = hidden


def down_kernel(ix_ref, h_ref, w0_ref, w1_ref, w2_ref, w3_ref, out_ref):
    rows = h_ref.shape[1]
    half = rows // 2
    hid = jnp.concatenate([h_ref[lax.rem(ix_ref[0] - s + 4, 4)] for s in range(4)], axis=1)
    blocks = []
    for b in range(5):
        weight = []
        for w_ref in (w0_ref, w1_ref, w2_ref, w3_ref):
            start = 2560 + b * 256
            weight.append(
                jnp.concatenate([w_ref[start : start + 128], w_ref[start + 128 : start + 256]], axis=1)
            )
        blocks.append(dot(hid, jnp.concatenate(weight, axis=0)))
    full = jnp.concatenate(blocks, axis=1)
    for y in range(4):
        own = full[:, y * 320 : (y + 1) * 320]
        out_ref[y, :rows] = own[:, :128].astype(BF)
        out_ref[y, rows : 2 * rows] = own[:, 128:256].astype(BF)
        last = own[:, 256:]
        out_ref[y, 2 * rows :] = jnp.concatenate([last[:half], last[half:]], axis=1).astype(BF)


def body(
    seq_x,
    z_gate,
    bc_in,
    conv_x,
    conv_bc,
    log_decay,
    skip_d,
    norm_gain,
    routes,
    route_gates,
    placement,
    gate_w,
    up_w,
    down_w,
):
    tokens, width = seq_x.shape
    heads = width // HEAD_DIM
    experts = placement.shape[0]
    slots = experts * PIECE
    ix = lax.axis_index("x").astype(jnp.int32)
    place = jnp.stack([lax.axis_index(NEAR), lax.axis_index("c"), lax.axis_index("zh")]).astype(jnp.int32)

    edge = kernel_call(edge_kernel, [((16, 640), BF)], seq_x.T, bc_in)
    rim = lax.ppermute(edge, CTX, [(i, i + 1) for i in range(31)])
    ixs = ix.reshape(1)
    own = (gate_w[0], up_w[0], down_w[0])
    pieces = dict(zip((1, 3, 2, 0), weight_pieces((1, 3, 2, 0), ixs, *own)))
    swapped = {s: lax.ppermute(pieces[s], "x", [(i, (i + s) % 4) for i in range(4)]) for s in (1, 3)}
    xs, bcs, run, turn, message = kernel_call(
        state_kernel,
        [
            ((tokens, width), F32),
            ((tokens, 2 * STATE), F32),
            ((tokens, STATE), F32),
            ((STATE, tokens), F32),
            ((width + 16, STATE), BF),
        ],
        seq_x.T,
        bc_in,
        rim,
        conv_x,
        conv_bc,
        log_decay.T,
        scratch=[pltpu.VMEM((STATE, tokens), F32)],
    )
    near = lax.all_gather(message, NEAR)
    near, swapped[1], swapped[3] = lax.optimization_barrier((near, swapped[1], swapped[3]))
    near_carried, near_log, group = kernel_call(
        near_kernel,
        [((width, STATE), F32), ((8, STATE), F32), ((width // 2 + 16, STATE), BF)],
        place,
        near,
        scalars=1,
        scratch=[pltpu.VMEM((width, STATE), BF)],
    )
    fars = lax.all_gather(group, "zh")
    turn, group, *owned = lax.optimization_barrier((turn, group, routes, placement))
    select = kernel_call(
        select_kernel, [((slots, 4 * tokens), BF)], owned[0].T, owned[1].reshape(1, experts)
    )
    y_in, z_in = pl.pallas_call(
        inner_kernel,
        out_shape=[jax.ShapeDtypeStruct((tokens, width), F32)] * 2,
        in_specs=[pl.BlockSpec(memory_space=pltpu.VMEM)] * 4
        + [pl.BlockSpec(memory_space=pltpu.SMEM), pl.BlockSpec(memory_space=pltpu.VMEM)],
        out_specs=[pl.BlockSpec(memory_space=pltpu.VMEM)] * 2,
        compiler_params=pltpu.CompilerParams(vmem_limit_bytes=20 << 20),
    )(xs, bcs, run, turn, skip_d, z_gate.T)
    far = kernel_call(far_kernel, [((width // 2, STATE), BF)], place, fars, scalars=1)
    other = lax.ppermute(far, "c", [(0, 1), (1, 0)])
    normed, outgoing = kernel_call(
        finish_kernel,
        [((width, tokens), BF), ((slots, LANES), BF)],
        place,
        far,
        other,
        near_carried,
        near_log,
        bcs,
        run,
        y_in,
        z_in,
        norm_gain.reshape(1, width),
        select,
        scalars=1,
        scratch=[pltpu.VMEM((width, STATE), BF)],
    )
    normed, *own = lax.optimization_barrier((normed, routes, placement))
    swapped[2] = lax.ppermute(pieces[2], "x", [(i, (i + 2) % 4) for i in range(4)])
    pick, half = kernel_call(
        pick_kernel,
        [((6 * tokens, slots), BF), ((tokens, 2), F32)],
        own[0].T,
        own[1].reshape(1, experts),
    )
    arrived = lax.all_to_all(outgoing.reshape(experts, PIECE, LANES), CTX, 0, 0, tiled=True)
    rows = (
        arrived[:, : GROUPS * HALF]
        .reshape(experts, GROUPS, HALF, LANES)
        .transpose(1, 0, 2, 3)
        .reshape(GROUPS * experts * HALF, LANES)
    )
    wide = lax.all_gather(rows, "y")
    count = 2 * experts * HALF
    weights = [pieces[0], swapped[1], swapped[2], swapped[3]]
    parts = kernel_call(gate_up_kernel, [((4, 2 * count, LANES), BF)], ixs, wide, *weights, scalars=1)
    parts = lax.all_to_all(parts, "x", 0, 0, tiled=True)
    hidden = kernel_call(hidden_kernel, [((4, count, LANES), BF)], parts)
    hiddens = lax.all_to_all(hidden, "x", 0, 0, tiled=True)
    downs = kernel_call(down_kernel, [((4, count * 5 // 2, LANES), BF)], ixs, hiddens, *weights, scalars=1)
    downs = lax.all_to_all(downs, "y", 0, 0, tiled=True)
    result = jnp.sum(downs.astype(F32), axis=0).astype(BF)
    result = result.reshape(GROUPS, experts, HALF, LANES).transpose(1, 0, 2, 3)
    result = jnp.pad(result.reshape(experts, GROUPS * HALF, LANES), ((0, 0), (0, 2), (0, 0)))
    returned = lax.all_to_all(result, CTX, 0, 0, tiled=True).reshape(slots, LANES)
    mixed = kernel_call(mix_kernel, [((width, tokens), BF)], pick, returned, route_gates.T, half)
    return (normed.T, mixed.T)


def solution(mesh):
    split = Mesh(mesh.devices.reshape(4, 4, 2, 4, 4), ("zh", "zl", "c", "x", "y"))
    placed = (
        P(CTX, EXP),
        P(CTX, EXP),
        P(CTX, None),
        P(None, EXP),
        P(),
        P(CTX, EXP),
        P(EXP),
        P(EXP),
        P(CTX, None),
        P(CTX, None),
        P(),
        P(CTX, None, EXP),
        P(CTX, None, EXP),
        P(CTX, EXP, None),
    )
    return jax.shard_map(
        body,
        mesh=split,
        in_specs=placed,
        out_specs=(P(CTX, EXP), P(CTX, EXP)),
        check_vma=False,
    )
```

```python
import functools

import jax
import jax.numpy as jnp
from jax import lax
from jax.experimental import pallas as pl
from jax.experimental.pallas import tpu as pltpu
from jax.sharding import Mesh
from jax.sharding import PartitionSpec as P

HEAD_DIM = 64
STATE = 128
CONV = 4
CTX = ("zh", "zl", "c")
EXP = ("x", "y")
NEAR = ("zl", "c")
LANES = 128
HALF = 6
GROUPS = 5
PIECE = 32

BF = jnp.bfloat16
F32 = jnp.float32


def dot(a, b):
    return jnp.dot(a, b, preferred_element_type=F32)


def kernel_call(kernel, outs, *operands, scalars=0, scratch=()):
    specs = [pl.BlockSpec(memory_space=pltpu.SMEM)] * scalars
    specs += [pl.BlockSpec(memory_space=pltpu.VMEM)] * (len(operands) - scalars)
    shapes = [jax.ShapeDtypeStruct(shape, kind) for shape, kind in outs]
    result = pl.pallas_call(
        kernel,
        out_shape=shapes,
        in_specs=specs,
        out_specs=[pl.BlockSpec(memory_space=pltpu.VMEM)] * len(outs),
        scratch_shapes=list(scratch),
        compiler_params=pltpu.CompilerParams(vmem_limit_bytes=20 << 20),
    )(*operands)
    return result[0] if len(outs) == 1 else result


def exact(a, b, dims=((1,), (0,))):
    return lax.dot_general(a, b, (dims, ((), ())), precision=lax.Precision.HIGHEST, preferred_element_type=F32)


def iota(shape, axis):
    return lax.broadcasted_iota(jnp.int32, shape, axis)


def silu(value):
    return value * jax.nn.sigmoid(value)


def turned(value):
    return value.astype(F32).T


def column(row):
    size = row.shape[1]
    hit = iota((size, size), 0) == iota((size, size), 1)
    return jnp.sum(jnp.where(hit, row.astype(F32), 0.0), axis=1, keepdims=True)


def edge_kernel(x_ref, bc_ref, out_ref):
    width, rows = x_ref.shape
    out_ref[:, :width] = turned(x_ref[...])[rows - 16 :].astype(BF)
    out_ref[:, width:384] = jnp.zeros((16, 384 - width), BF)
    out_ref[:, 384:] = bc_ref[rows - 16 :]


def pick_kernel(routes_ref, row_ref, pick_ref, half_ref):
    tokens = routes_ref.shape[1]
    experts = row_ref.shape[1]
    slots = experts * PIECE
    hot = [
        (column(routes_ref[k : k + 1]) == iota((tokens, experts), 1).astype(F32)).astype(F32)
        for k in range(2)
    ]
    earlier = (iota((tokens, tokens), 0) > iota((tokens, tokens), 1)).astype(BF)
    before = dot(earlier, (hot[0] + hot[1]).astype(BF))
    for k in range(2):
        rank = jnp.sum(hot[k] * before, axis=1, keepdims=True).astype(jnp.int32)
        owner = jnp.sum(hot[k] * row_ref[...].astype(F32), axis=1, keepdims=True).astype(jnp.int32)
        half = (rank >= HALF).astype(jnp.int32)
        base = owner * PIECE + rank - HALF * half
        half_ref[:, k : k + 1] = half.astype(F32)
        places = iota((tokens, slots), 1)
        for plane, where in enumerate((base + HALF * half, base + HALF * (half + 2), base + 4 * HALF)):
            start = (plane * 2 + k) * tokens
            pick_ref[start : start + tokens] = (places == where).astype(F32).astype(BF)


def select_kernel(routes_ref, row_ref, select_ref):
    tokens = routes_ref.shape[1]
    experts = row_ref.shape[1]
    slots = experts * PIECE
    hot = [(routes_ref[k : k + 1] == iota((experts, tokens), 0)).astype(F32) for k in range(2)]
    later = (iota((tokens, tokens), 0) < iota((tokens, tokens), 1)).astype(BF)
    before = dot((hot[0] + hot[1]).astype(BF), later)
    places = iota((slots, tokens), 0)
    planes = [jnp.zeros((slots, tokens), F32)] * 4
    owned = column(row_ref[...])
    for k in range(2):
        rank = jnp.sum(hot[k] * before, axis=0, keepdims=True).astype(jnp.int32)
        owner = jnp.sum(hot[k] * owned, axis=0, keepdims=True).astype(jnp.int32)
        half = (rank >= HALF).astype(jnp.int32)
        base = owner * PIECE + rank - HALF * half
        last = base + 4 * HALF
        wheres = (
            base + HALF * half,
            base + HALF * (half + 2),
            jnp.where(half == 0, last, -1),
            jnp.where(half == 1, last, -1),
        )
        planes = [p + (places == w).astype(F32) for p, w in zip(planes, wheres)]
    for plane in range(4):
        select_ref[:, plane * tokens : (plane + 1) * tokens] = planes[plane].astype(BF)


def spread(columns, heads):
    rows = columns.shape[0]
    return jnp.concatenate(
        [jnp.broadcast_to(columns[:, h : h + 1], (rows, HEAD_DIM)) for h in range(heads)], axis=1
    )


def write_logs(ref, start, logs):
    high = logs.astype(BF).astype(F32)
    places = iota((16, STATE), 0)
    tail = jnp.where(places == 0, high, jnp.where(places == 1, logs - high, 0.0))
    ref[start : start + 16] = tail.astype(BF)


def read_logs(tail):
    tail = tail.astype(F32)
    return tail[0:1] + tail[1:2]


def state_kernel(x_ref, bc_ref, rim_ref, cx_ref, cbc_ref, decay_ref, xs_ref, bcs_ref, run_ref, turn_ref, msg_ref, scratch):
    width, tokens = x_ref.shape
    heads = width // HEAD_DIM

    def conv(rim, value, taps):
        long = jnp.concatenate([rim.astype(F32), value], axis=0)
        total = taps[CONV - 1 : CONV] * long[16:]
        for back in range(1, CONV):
            total += taps[CONV - 1 - back : CONV - back] * pltpu.roll(long, back, 0)[16:]
        return silu(total)

    parts = []
    for start in range(0, width, LANES):
        stop = min(start + LANES, width)
        parts.append(conv(rim_ref[:, start:stop], turned(x_ref[start:stop]), cx_ref[:, start:stop]))
    xs = jnp.concatenate(parts, axis=1)
    bcs = conv(rim_ref[:, 384:], bc_ref[...].astype(F32), cbc_ref[...])
    lower = (iota((tokens, tokens), 0) >= iota((tokens, tokens), 1)).astype(F32)
    scratch[...] = jnp.zeros(scratch.shape, F32)
    scratch[:heads] = decay_ref[...]
    run = exact(lower, scratch[...], ((1,), (1,)))
    last = run[tokens - 1 : tokens]
    tails = jnp.exp(last - run)
    state = exact(xs * spread(tails, heads), bcs[:, :STATE], ((0,), (0,)))
    xs_ref[...] = xs
    bcs_ref[...] = bcs
    run_ref[...] = run
    turn_ref[...] = exact(scratch[...], lower, ((1,), (1,)))
    msg_ref[:width] = state.astype(BF)
    write_logs(msg_ref, width, last)


def inner_kernel(xs_ref, bcs_ref, run_ref, turn_ref, skip_ref, z_ref, y_ref, z_out_ref):
    tokens, width = xs_ref.shape
    lower = iota((tokens, tokens), 0) >= iota((tokens, tokens), 1)
    scores = exact(bcs_ref[:, STATE:], bcs_ref[:, :STATE], ((1,), (1,)))
    outs = []
    for h in range(width // HEAD_DIM):
        gaps = run_ref[:, h : h + 1] - turn_ref[h : h + 1]
        weight = jnp.where(lower, jnp.exp(jnp.where(lower, gaps, 0.0)), 0.0) * scores
        x = xs_ref[:, h * HEAD_DIM : (h + 1) * HEAD_DIM]
        outs.append(exact(weight, x) + skip_ref[h] * x)
    y_ref[...] = jnp.concatenate(outs, axis=1)
    z_out_ref[...] = silu(turned(z_ref[...]))


def near_kernel(place_ref, near_ref, carried_ref, log_ref, msg_ref, scratch):
    count, rows, _ = near_ref.shape
    rows -= 16
    heads = rows // HEAD_DIM
    total = [jnp.zeros((HEAD_DIM, STATE), F32)] * heads
    kept = total
    log = jnp.zeros((1, STATE), F32)
    kept_log = log
    for j in range(count):
        own = place_ref[0] == j
        kept = [jnp.where(own, t, k) for t, k in zip(total, kept)]
        kept_log = jnp.where(own, log, kept_log)
        step = read_logs(near_ref[j, rows:])
        factor = jnp.exp(step)
        log = log + step
        total = [
            factor[:, h : h + 1] * total[h] + near_ref[j, h * HEAD_DIM : (h + 1) * HEAD_DIM].astype(F32)
            for h in range(heads)
        ]
    for h in range(heads):
        carried_ref[h * HEAD_DIM : (h + 1) * HEAD_DIM] = kept[h]
        scratch[h * HEAD_DIM : (h + 1) * HEAD_DIM] = total[h].astype(BF)
    log_ref[...] = jnp.broadcast_to(kept_log, log_ref.shape)
    part = rows // 2
    msg_ref[:part] = scratch[pl.ds(pl.multiple_of(place_ref[1] * part, 32), part)]
    write_logs(msg_ref, part, log)


def far_kernel(place_ref, far_ref, out_ref):
    part = out_ref.shape[0]
    units = part // 32
    lanes = iota((1, STATE), 1)
    total = [jnp.zeros((32, STATE), F32)] * units
    for g in range(far_ref.shape[0] - 1):
        factor = jnp.exp(read_logs(far_ref[g, part:]))
        earlier = g < place_ref[2]
        for u in range(units):
            head = (place_ref[1] * units + u) // 2
            one = jnp.sum(jnp.where(lanes == head, factor, 0.0), axis=1, keepdims=True)
            state = far_ref[g, u * 32 : (u + 1) * 32].astype(F32)
            total[u] = jnp.where(earlier, one * total[u] + state, total[u])
    for u in range(units):
        out_ref[u * 32 : (u + 1) * 32] = total[u].astype(BF)


def finish_kernel(
    place_ref, own_ref, other_ref, near_ref, log_ref, bcs_ref, run_ref, y_ref, z_ref, gain_ref, select_ref,
    normed_ref, out_ref, scratch,
):
    part = own_ref.shape[0]
    tokens, width = y_ref.shape
    heads = width // HEAD_DIM
    core = place_ref[1]
    scratch[pl.ds(pl.multiple_of(core * part, 32), part)] = own_ref[...]
    scratch[pl.ds(pl.multiple_of((1 - core) * part, 32), part)] = other_ref[...]
    factor = jnp.exp(log_ref[0:1])
    carried = jnp.concatenate(
        [
            near_ref[h * HEAD_DIM : (h + 1) * HEAD_DIM]
            + factor[:, h : h + 1] * scratch[h * HEAD_DIM : (h + 1) * HEAD_DIM].astype(F32)
            for h in range(heads)
        ],
        axis=0,
    )
    outer = exact(bcs_ref[:, STATE:], carried, ((1,), (1,))) * spread(jnp.exp(run_ref[...]), heads)
    gated = (y_ref[...] + outer) * z_ref[...]
    square = gated * gated
    scales = jnp.concatenate(
        [
            jnp.broadcast_to(
                lax.rsqrt(
                    jnp.mean(square[:, h * HEAD_DIM : (h + 1) * HEAD_DIM], axis=1, keepdims=True) + 1e-05
                ),
                (tokens, HEAD_DIM),
            )
            for h in range(heads)
        ],
        axis=1,
    )
    normed = (gated * scales * gain_ref[...]).astype(BF)
    normed_ref[...] = turned(normed).astype(BF)
    blank = jnp.zeros((tokens, 64), BF)
    planes = jnp.concatenate(
        [
            normed[:, :128],
            normed[:, 128:256],
            jnp.concatenate([normed[:, 256:], blank], axis=1),
            jnp.concatenate([blank, normed[:, 256:]], axis=1),
        ],
        axis=0,
    )
    out_ref[...] = dot(select_ref[...], planes).astype(BF)


def piece_kernel(steps, ix_ref, gate_ref, up_ref, down_ref, *rest):
    outs, (held, in_sems, out_sems) = rest[: len(steps)], rest[len(steps) :]
    span = gate_ref.shape[0] // 4
    arrivals = []
    for i, step in enumerate(steps):
        block = pl.multiple_of(lax.rem(ix_ref[0] + step, 4) * span, span)
        pairs = [
            (gate_ref.at[pl.ds(block, span)], held.at[i, pl.ds(0, span)]),
            (up_ref.at[pl.ds(block, span)], held.at[i, pl.ds(span, span)]),
        ]
        for b in range(span // LANES):
            pairs.append(
                (
                    down_ref.at[:, pl.ds(pl.multiple_of(block + b * LANES, LANES), LANES)],
                    held.at[i, pl.ds(2 * span + b * LANES, LANES)],
                )
            )
        arrivals.append(
            [pltpu.make_async_copy(p, q, in_sems.at[i, n]) for n, (p, q) in enumerate(pairs)]
        )
    for copies in arrivals:
        for copy in copies:
            copy.start()
    departures = []
    for i, copies in enumerate(arrivals):
        for copy in copies:
            copy.wait()
        departures.append(pltpu.make_async_copy(held.at[i], outs[i], out_sems.at[i]))
        departures[i].start()
    for copy in departures:
        copy.wait()


def weight_pieces(steps, ix, gate, up, down):
    span = gate.shape[0] // 4
    count = len(steps)
    whole = pl.BlockSpec(memory_space=pltpu.HBM)
    return pl.pallas_call(
        functools.partial(piece_kernel, steps),
        out_shape=[jax.ShapeDtypeStruct((3 * span, LANES), BF)] * count,
        in_specs=[pl.BlockSpec(memory_space=pltpu.SMEM), whole, whole, whole],
        out_specs=[whole] * count,
        scratch_shapes=[
            pltpu.VMEM((count, 3 * span, LANES), BF),
            pltpu.SemaphoreType.DMA((count, 2 + span // LANES)),
            pltpu.SemaphoreType.DMA((count,)),
        ],
        compiler_params=pltpu.CompilerParams(vmem_limit_bytes=60 << 20),
    )(ix, gate, up, down)


def mix_kernel(pick_ref, rows_ref, gates_ref, half_ref, out_ref):
    tokens = gates_ref.shape[1]
    picked = dot(pick_ref[...], rows_ref[...])
    totals = [0.0, 0.0, 0.0]
    for k in range(2):
        gate = column(gates_ref[k : k + 1])
        for plane in range(3):
            start = (plane * 2 + k) * tokens
            one = picked[start : start + tokens]
            if plane == 2:
                one = jnp.where(half_ref[:, k : k + 1] > 0.5, one[:, 64:], one[:, :64])
            totals[plane] = totals[plane] + gate * one
    for plane in range(3):
        size = min(LANES, out_ref.shape[0] - plane * LANES)
        out_ref[plane * LANES : plane * LANES + size] = totals[plane].T.astype(BF)


def gate_up_kernel(ix_ref, g_ref, gate_ref, up_ref, w1_ref, w2_ref, w3_ref, out_ref):
    rows = 2 * 192
    wide = [jnp.concatenate([g_ref[y, :rows], g_ref[y, rows : 2 * rows]], axis=1) for y in range(4)]
    slim = []
    for y in range(4):
        packed = g_ref[y, 2 * rows :]
        slim.append(jnp.concatenate([packed[:, :64], packed[:, 64:]], axis=0))
    pairs = [jnp.concatenate([slim[0], slim[1]], axis=1), jnp.concatenate([slim[2], slim[3]], axis=1)]
    span = gate_ref.shape[0]
    for s, w_ref in enumerate((None, w1_ref, w2_ref, w3_ref)):
        target = lax.rem(ix_ref[0] - s + 4, 4)

        def weight(start, size):
            if w_ref is None:
                return jnp.concatenate(
                    [gate_ref[start : start + size], up_ref[start : start + size]], axis=1
                )
            return jnp.concatenate(
                [w_ref[start : start + size], w_ref[span + start : span + start + size]], axis=1
            )

        total = dot(wide[0], weight(0, 256))
        for y in range(1, 4):
            total += dot(wide[y], weight(y * 320, 256))
        for p in range(2):
            low, high = weight(p * 640 + 256, 64), weight(p * 640 + 576, 64)
            total += dot(pairs[p], jnp.concatenate([low, high], axis=0))
        out_ref[target, :rows] = total[:, :LANES].astype(BF)
        out_ref[target, rows:] = total[:, LANES:].astype(BF)


def hidden_kernel(p_ref, out_ref):
    rows = p_ref.shape[1] // 2
    total = p_ref[0].astype(F32)
    for i in range(1, 4):
        total += p_ref[i].astype(F32)
    gate, up = total[:rows], total[rows:]
    hidden = (silu(gate) * up).astype(BF)
    for i in range(4):
        out_ref[i] = hidden


def down_kernel(ix_ref, h_ref, down_ref, w1_ref, w2_ref, w3_ref, out_ref):
    rows = h_ref.shape[1]
    half = rows // 2
    hid = jnp.concatenate([h_ref[lax.rem(ix_ref[0] - s + 4, 4)] for s in range(4)], axis=1)
    blocks = []
    for b in range(5):
        start = b * 256
        weight = [down_ref[:, start : start + 256]]
        for w_ref in (w1_ref, w2_ref, w3_ref):
            weight.append(
                jnp.concatenate([w_ref[start : start + 128], w_ref[start + 128 : start + 256]], axis=1)
            )
        blocks.append(dot(hid, jnp.concatenate(weight, axis=0)))
    full = jnp.concatenate(blocks, axis=1)
    for y in range(4):
        own = full[:, y * 320 : (y + 1) * 320]
        out_ref[y, :rows] = own[:, :128].astype(BF)
        out_ref[y, rows : 2 * rows] = own[:, 128:256].astype(BF)
        last = own[:, 256:]
        out_ref[y, 2 * rows :] = jnp.concatenate([last[:half], last[half:]], axis=1).astype(BF)


def expert_call(kernel, shape, ix, rows, own, own_specs, pieces, piece_spec):
    whole = pl.BlockSpec(rows.shape, lambda i, b: (0, 0, 0))
    return pl.pallas_call(
        kernel,
        out_shape=jax.ShapeDtypeStruct(shape, BF),
        grid_spec=pltpu.PrefetchScalarGridSpec(
            num_scalar_prefetch=1,
            grid=(1,),
            in_specs=[whole, *own_specs] + [piece_spec] * len(pieces),
            out_specs=pl.BlockSpec(shape, lambda i, b: (0, 0, 0)),
        ),
        compiler_params=pltpu.CompilerParams(vmem_limit_bytes=24 << 20),
    )(ix, rows, *own, *pieces)


def body(
    seq_x,
    z_gate,
    bc_in,
    conv_x,
    conv_bc,
    log_decay,
    skip_d,
    norm_gain,
    routes,
    route_gates,
    placement,
    gate_w,
    up_w,
    down_w,
):
    tokens, width = seq_x.shape
    heads = width // HEAD_DIM
    experts = placement.shape[0]
    slots = experts * PIECE
    ix = lax.axis_index("x").astype(jnp.int32)
    place = jnp.stack([lax.axis_index(NEAR), lax.axis_index("c"), lax.axis_index("zh")]).astype(jnp.int32)

    edge = kernel_call(edge_kernel, [((16, 640), BF)], seq_x.T, bc_in)
    rim = lax.ppermute(edge, CTX, [(i, i + 1) for i in range(31)])
    ixs = ix.reshape(1)
    own = (gate_w[0], up_w[0], down_w[0])
    pieces = dict(zip((1, 3, 2), weight_pieces((1, 3, 2), ixs, *own)))
    swapped = {s: lax.ppermute(pieces[s], "x", [(i, (i + s) % 4) for i in range(4)]) for s in (1, 3)}
    xs, bcs, run, turn, message = kernel_call(
        state_kernel,
        [
            ((tokens, width), F32),
            ((tokens, 2 * STATE), F32),
            ((tokens, STATE), F32),
            ((STATE, tokens), F32),
            ((width + 16, STATE), BF),
        ],
        seq_x.T,
        bc_in,
        rim,
        conv_x,
        conv_bc,
        log_decay.T,
        scratch=[pltpu.VMEM((STATE, tokens), F32)],
    )
    near = lax.all_gather(message, NEAR)
    near, swapped[1], swapped[3] = lax.optimization_barrier((near, swapped[1], swapped[3]))
    near_carried, near_log, group = kernel_call(
        near_kernel,
        [((width, STATE), F32), ((8, STATE), F32), ((width // 2 + 16, STATE), BF)],
        place,
        near,
        scalars=1,
        scratch=[pltpu.VMEM((width, STATE), BF)],
    )
    fars = lax.all_gather(group, "zh")
    turn, group, *owned = lax.optimization_barrier((turn, group, routes, placement))
    select = kernel_call(
        select_kernel, [((slots, 4 * tokens), BF)], owned[0].T, owned[1].reshape(1, experts)
    )
    y_in, z_in = pl.pallas_call(
        inner_kernel,
        out_shape=[jax.ShapeDtypeStruct((tokens, width), F32)] * 2,
        in_specs=[pl.BlockSpec(memory_space=pltpu.VMEM)] * 4
        + [pl.BlockSpec(memory_space=pltpu.SMEM), pl.BlockSpec(memory_space=pltpu.VMEM)],
        out_specs=[pl.BlockSpec(memory_space=pltpu.VMEM)] * 2,
        compiler_params=pltpu.CompilerParams(vmem_limit_bytes=20 << 20),
    )(xs, bcs, run, turn, skip_d, z_gate.T)
    far = kernel_call(far_kernel, [((width // 2, STATE), BF)], place, fars, scalars=1)
    other = lax.ppermute(far, "c", [(0, 1), (1, 0)])
    normed, outgoing = kernel_call(
        finish_kernel,
        [((width, tokens), BF), ((slots, LANES), BF)],
        place,
        far,
        other,
        near_carried,
        near_log,
        bcs,
        run,
        y_in,
        z_in,
        norm_gain.reshape(1, width),
        select,
        scalars=1,
        scratch=[pltpu.VMEM((width, STATE), BF)],
    )
    normed, *own = lax.optimization_barrier((normed, routes, placement))
    swapped[2] = lax.ppermute(pieces[2], "x", [(i, (i + 2) % 4) for i in range(4)])
    pick, half = kernel_call(
        pick_kernel,
        [((6 * tokens, slots), BF), ((tokens, 2), F32)],
        own[0].T,
        own[1].reshape(1, experts),
    )
    arrived = lax.all_to_all(outgoing.reshape(experts, PIECE, LANES), CTX, 0, 0, tiled=True)
    rows = (
        arrived[:, : GROUPS * HALF]
        .reshape(experts, GROUPS, HALF, LANES)
        .transpose(1, 0, 2, 3)
        .reshape(GROUPS * experts * HALF, LANES)
    )
    wide = lax.all_gather(rows, "y")
    count = 2 * experts * HALF
    weights = [swapped[1], swapped[2], swapped[3]]
    span = gate_w.shape[1] // 4
    across = pl.BlockSpec((span, LANES), lambda i, b: (b[0], 0))
    along = pl.BlockSpec((LANES, span), lambda i, b: (0, b[0]))
    parts = expert_call(
        gate_up_kernel,
        (4, 2 * count, LANES),
        ixs,
        wide,
        (gate_w[0], up_w[0]),
        (across, across),
        weights,
        pl.BlockSpec((2 * span, LANES), lambda i, b: (0, 0)),
    )
    parts = lax.all_to_all(parts, "x", 0, 0, tiled=True)
    hidden = kernel_call(hidden_kernel, [((4, count, LANES), BF)], parts)
    hiddens = lax.all_to_all(hidden, "x", 0, 0, tiled=True)
    downs = expert_call(
        down_kernel,
        (4, count * 5 // 2, LANES),
        ixs,
        hiddens,
        (down_w[0],),
        (along,),
        weights,
        pl.BlockSpec((span, LANES), lambda i, b: (2, 0)),
    )
    downs = lax.all_to_all(downs, "y", 0, 0, tiled=True)
    result = jnp.sum(downs.astype(F32), axis=0).astype(BF)
    result = result.reshape(GROUPS, experts, HALF, LANES).transpose(1, 0, 2, 3)
    result = jnp.pad(result.reshape(experts, GROUPS * HALF, LANES), ((0, 0), (0, 2), (0, 0)))
    returned = lax.all_to_all(result, CTX, 0, 0, tiled=True).reshape(slots, LANES)
    mixed = kernel_call(mix_kernel, [((width, tokens), BF)], pick, returned, route_gates.T, half)
    return (normed.T, mixed.T)


def solution(mesh):
    split = Mesh(mesh.devices.reshape(4, 4, 2, 4, 4), ("zh", "zl", "c", "x", "y"))
    placed = (
        P(CTX, EXP),
        P(CTX, EXP),
        P(CTX, None),
        P(None, EXP),
        P(),
        P(CTX, EXP),
        P(EXP),
        P(EXP),
        P(CTX, None),
        P(CTX, None),
        P(),
        P(CTX, None, EXP),
        P(CTX, None, EXP),
        P(CTX, EXP, None),
    )
    return jax.shard_map(
        body,
        mesh=split,
        in_specs=placed,
        out_specs=(P(CTX, EXP), P(CTX, EXP)),
        check_vma=False,
    )
```

```python
import functools

import jax
import jax.numpy as jnp
from jax import lax
from jax.experimental import pallas as pl
from jax.experimental.pallas import tpu as pltpu
from jax.sharding import Mesh
from jax.sharding import PartitionSpec as P

HEAD_DIM = 64
STATE = 128
CONV = 4
CTX = ("zh", "zl", "c")
EXP = ("x", "y")
NEAR = ("zl", "c")
LANES = 128
HALF = 6
GROUPS = 5
PIECE = 32

BF = jnp.bfloat16
F32 = jnp.float32


def dot(a, b):
    return jnp.dot(a, b, preferred_element_type=F32)


def kernel_call(kernel, outs, *operands, scalars=0, scratch=()):
    specs = [pl.BlockSpec(memory_space=pltpu.SMEM)] * scalars
    specs += [pl.BlockSpec(memory_space=pltpu.VMEM)] * (len(operands) - scalars)
    shapes = [jax.ShapeDtypeStruct(shape, kind) for shape, kind in outs]
    result = pl.pallas_call(
        kernel,
        out_shape=shapes,
        in_specs=specs,
        out_specs=[pl.BlockSpec(memory_space=pltpu.VMEM)] * len(outs),
        scratch_shapes=list(scratch),
        compiler_params=pltpu.CompilerParams(vmem_limit_bytes=20 << 20),
    )(*operands)
    return result[0] if len(outs) == 1 else result


def exact(a, b, dims=((1,), (0,))):
    return lax.dot_general(a, b, (dims, ((), ())), precision=lax.Precision.HIGHEST, preferred_element_type=F32)


def iota(shape, axis):
    return lax.broadcasted_iota(jnp.int32, shape, axis)


def silu(value):
    return value * jax.nn.sigmoid(value)


def turned(value):
    return value.astype(F32).T


def column(row):
    size = row.shape[1]
    hit = iota((size, size), 0) == iota((size, size), 1)
    return jnp.sum(jnp.where(hit, row.astype(F32), 0.0), axis=1, keepdims=True)


def edge_kernel(x_ref, bc_ref, out_ref):
    width, rows = x_ref.shape
    out_ref[:, :width] = turned(x_ref[...])[rows - 16 :].astype(BF)
    out_ref[:, width:384] = jnp.zeros((16, 384 - width), BF)
    out_ref[:, 384:] = bc_ref[rows - 16 :]


def pick_kernel(routes_ref, row_ref, pick_ref, half_ref):
    tokens = routes_ref.shape[1]
    experts = row_ref.shape[1]
    slots = experts * PIECE
    hot = [
        (column(routes_ref[k : k + 1]) == iota((tokens, experts), 1).astype(F32)).astype(F32)
        for k in range(2)
    ]
    earlier = (iota((tokens, tokens), 0) > iota((tokens, tokens), 1)).astype(BF)
    before = dot(earlier, (hot[0] + hot[1]).astype(BF))
    for k in range(2):
        rank = jnp.sum(hot[k] * before, axis=1, keepdims=True).astype(jnp.int32)
        owner = jnp.sum(hot[k] * row_ref[...].astype(F32), axis=1, keepdims=True).astype(jnp.int32)
        half = (rank >= HALF).astype(jnp.int32)
        base = owner * PIECE + rank - HALF * half
        half_ref[:, k : k + 1] = half.astype(F32)
        places = iota((tokens, slots), 1)
        for plane, where in enumerate((base + HALF * half, base + HALF * (half + 2), base + 4 * HALF)):
            start = (plane * 2 + k) * tokens
            pick_ref[start : start + tokens] = (places == where).astype(F32).astype(BF)


def select_kernel(routes_ref, row_ref, select_ref):
    tokens = routes_ref.shape[1]
    experts = row_ref.shape[1]
    slots = experts * PIECE
    hot = [(routes_ref[k : k + 1] == iota((experts, tokens), 0)).astype(F32) for k in range(2)]
    later = (iota((tokens, tokens), 0) < iota((tokens, tokens), 1)).astype(BF)
    before = dot((hot[0] + hot[1]).astype(BF), later)
    places = iota((slots, tokens), 0)
    planes = [jnp.zeros((slots, tokens), F32)] * 4
    owned = column(row_ref[...])
    for k in range(2):
        rank = jnp.sum(hot[k] * before, axis=0, keepdims=True).astype(jnp.int32)
        owner = jnp.sum(hot[k] * owned, axis=0, keepdims=True).astype(jnp.int32)
        half = (rank >= HALF).astype(jnp.int32)
        base = owner * PIECE + rank - HALF * half
        last = base + 4 * HALF
        wheres = (
            base + HALF * half,
            base + HALF * (half + 2),
            jnp.where(half == 0, last, -1),
            jnp.where(half == 1, last, -1),
        )
        planes = [p + (places == w).astype(F32) for p, w in zip(planes, wheres)]
    for plane in range(4):
        select_ref[:, plane * tokens : (plane + 1) * tokens] = planes[plane].astype(BF)


def spread(columns, heads):
    rows = columns.shape[0]
    return jnp.concatenate(
        [jnp.broadcast_to(columns[:, h : h + 1], (rows, HEAD_DIM)) for h in range(heads)], axis=1
    )


def write_logs(ref, start, logs):
    high = logs.astype(BF).astype(F32)
    places = iota((16, STATE), 0)
    tail = jnp.where(places == 0, high, jnp.where(places == 1, logs - high, 0.0))
    ref[start : start + 16] = tail.astype(BF)


def read_logs(tail):
    tail = tail.astype(F32)
    return tail[0:1] + tail[1:2]


def state_kernel(x_ref, bc_ref, rim_ref, cx_ref, cbc_ref, decay_ref, xs_ref, bcs_ref, run_ref, turn_ref, msg_ref, scratch):
    width, tokens = x_ref.shape
    heads = width // HEAD_DIM

    def conv(rim, value, taps):
        long = jnp.concatenate([rim.astype(F32), value], axis=0)
        total = taps[CONV - 1 : CONV] * long[16:]
        for back in range(1, CONV):
            total += taps[CONV - 1 - back : CONV - back] * pltpu.roll(long, back, 0)[16:]
        return silu(total)

    parts = []
    for start in range(0, width, LANES):
        stop = min(start + LANES, width)
        parts.append(conv(rim_ref[:, start:stop], turned(x_ref[start:stop]), cx_ref[:, start:stop]))
    xs = jnp.concatenate(parts, axis=1)
    bcs = conv(rim_ref[:, 384:], bc_ref[...].astype(F32), cbc_ref[...])
    lower = (iota((tokens, tokens), 0) >= iota((tokens, tokens), 1)).astype(F32)
    scratch[...] = jnp.zeros(scratch.shape, F32)
    scratch[:heads] = decay_ref[...]
    run = exact(lower, scratch[...], ((1,), (1,)))
    last = run[tokens - 1 : tokens]
    tails = jnp.exp(last - run)
    state = exact(xs * spread(tails, heads), bcs[:, :STATE], ((0,), (0,)))
    xs_ref[...] = xs
    bcs_ref[...] = bcs
    run_ref[...] = run
    turn_ref[...] = exact(scratch[...], lower, ((1,), (1,)))
    msg_ref[:width] = state.astype(BF)
    write_logs(msg_ref, width, last)


def inner_kernel(xs_ref, bcs_ref, run_ref, turn_ref, skip_ref, z_ref, y_ref, z_out_ref):
    tokens, width = xs_ref.shape
    lower = iota((tokens, tokens), 0) >= iota((tokens, tokens), 1)
    scores = exact(bcs_ref[:, STATE:], bcs_ref[:, :STATE], ((1,), (1,)))
    outs = []
    for h in range(width // HEAD_DIM):
        gaps = run_ref[:, h : h + 1] - turn_ref[h : h + 1]
        weight = jnp.where(lower, jnp.exp(jnp.where(lower, gaps, 0.0)), 0.0) * scores
        x = xs_ref[:, h * HEAD_DIM : (h + 1) * HEAD_DIM]
        outs.append(exact(weight, x) + skip_ref[h] * x)
    y_ref[...] = jnp.concatenate(outs, axis=1)
    z_out_ref[...] = silu(turned(z_ref[...]))


def near_kernel(place_ref, near_ref, carried_ref, log_ref, msg_ref, scratch):
    count, rows, _ = near_ref.shape
    rows -= 16
    heads = rows // HEAD_DIM
    total = [jnp.zeros((HEAD_DIM, STATE), F32)] * heads
    kept = total
    log = jnp.zeros((1, STATE), F32)
    kept_log = log
    for j in range(count):
        own = place_ref[0] == j
        kept = [jnp.where(own, t, k) for t, k in zip(total, kept)]
        kept_log = jnp.where(own, log, kept_log)
        step = read_logs(near_ref[j, rows:])
        factor = jnp.exp(step)
        log = log + step
        total = [
            factor[:, h : h + 1] * total[h] + near_ref[j, h * HEAD_DIM : (h + 1) * HEAD_DIM].astype(F32)
            for h in range(heads)
        ]
    for h in range(heads):
        carried_ref[h * HEAD_DIM : (h + 1) * HEAD_DIM] = kept[h]
        scratch[h * HEAD_DIM : (h + 1) * HEAD_DIM] = total[h].astype(BF)
    log_ref[...] = jnp.broadcast_to(kept_log, log_ref.shape)
    part = rows // 2
    msg_ref[:part] = scratch[pl.ds(pl.multiple_of(place_ref[1] * part, 32), part)]
    write_logs(msg_ref, part, log)


def far_kernel(place_ref, far_ref, out_ref):
    part = out_ref.shape[0]
    units = part // 32
    lanes = iota((1, STATE), 1)
    total = [jnp.zeros((32, STATE), F32)] * units
    for g in range(far_ref.shape[0] - 1):
        factor = jnp.exp(read_logs(far_ref[g, part:]))
        earlier = g < place_ref[2]
        for u in range(units):
            head = (place_ref[1] * units + u) // 2
            one = jnp.sum(jnp.where(lanes == head, factor, 0.0), axis=1, keepdims=True)
            state = far_ref[g, u * 32 : (u + 1) * 32].astype(F32)
            total[u] = jnp.where(earlier, one * total[u] + state, total[u])
    for u in range(units):
        out_ref[u * 32 : (u + 1) * 32] = total[u].astype(BF)


def finish_kernel(
    place_ref, own_ref, other_ref, near_ref, log_ref, bcs_ref, run_ref, y_ref, z_ref, gain_ref, select_ref,
    normed_ref, out_ref, scratch,
):
    part = own_ref.shape[0]
    tokens, width = y_ref.shape
    heads = width // HEAD_DIM
    core = place_ref[1]
    scratch[pl.ds(pl.multiple_of(core * part, 32), part)] = own_ref[...]
    scratch[pl.ds(pl.multiple_of((1 - core) * part, 32), part)] = other_ref[...]
    factor = jnp.exp(log_ref[0:1])
    carried = jnp.concatenate(
        [
            near_ref[h * HEAD_DIM : (h + 1) * HEAD_DIM]
            + factor[:, h : h + 1] * scratch[h * HEAD_DIM : (h + 1) * HEAD_DIM].astype(F32)
            for h in range(heads)
        ],
        axis=0,
    )
    outer = exact(bcs_ref[:, STATE:], carried, ((1,), (1,))) * spread(jnp.exp(run_ref[...]), heads)
    gated = (y_ref[...] + outer) * z_ref[...]
    square = gated * gated
    scales = jnp.concatenate(
        [
            jnp.broadcast_to(
                lax.rsqrt(
                    jnp.mean(square[:, h * HEAD_DIM : (h + 1) * HEAD_DIM], axis=1, keepdims=True) + 1e-05
                ),
                (tokens, HEAD_DIM),
            )
            for h in range(heads)
        ],
        axis=1,
    )
    normed = (gated * scales * gain_ref[...]).astype(BF)
    normed_ref[...] = turned(normed).astype(BF)
    blank = jnp.zeros((tokens, 64), BF)
    planes = jnp.concatenate(
        [
            normed[:, :128],
            normed[:, 128:256],
            jnp.concatenate([normed[:, 256:], blank], axis=1),
            jnp.concatenate([blank, normed[:, 256:]], axis=1),
        ],
        axis=0,
    )
    out_ref[...] = dot(select_ref[...], planes).astype(BF)


def piece_kernel(steps, ix_ref, gate_ref, up_ref, down_ref, *rest):
    outs, (held, in_sems, out_sems) = rest[: len(steps)], rest[len(steps) :]
    span = gate_ref.shape[0] // 4
    arrivals = []
    for i, step in enumerate(steps):
        block = pl.multiple_of(lax.rem(ix_ref[0] + step, 4) * span, span)
        pairs = [
            (gate_ref.at[pl.ds(block, span)], held.at[i, pl.ds(0, span)]),
            (up_ref.at[pl.ds(block, span)], held.at[i, pl.ds(span, span)]),
        ]
        for b in range(span // LANES):
            pairs.append(
                (
                    down_ref.at[:, pl.ds(pl.multiple_of(block + b * LANES, LANES), LANES)],
                    held.at[i, pl.ds(2 * span + b * LANES, LANES)],
                )
            )
        arrivals.append(
            [pltpu.make_async_copy(p, q, in_sems.at[i, n]) for n, (p, q) in enumerate(pairs)]
        )
    for copies in arrivals:
        for copy in copies:
            copy.start()
    departures = []
    for i, copies in enumerate(arrivals):
        for copy in copies:
            copy.wait()
        departures.append(pltpu.make_async_copy(held.at[i], outs[i], out_sems.at[i]))
        departures[i].start()
    for copy in departures:
        copy.wait()


def weight_pieces(steps, ix, gate, up, down):
    span = gate.shape[0] // 4
    count = len(steps)
    whole = pl.BlockSpec(memory_space=pltpu.HBM)
    return pl.pallas_call(
        functools.partial(piece_kernel, steps),
        out_shape=[jax.ShapeDtypeStruct((3 * span, LANES), BF)] * count,
        in_specs=[pl.BlockSpec(memory_space=pltpu.SMEM), whole, whole, whole],
        out_specs=[whole] * count,
        scratch_shapes=[
            pltpu.VMEM((count, 3 * span, LANES), BF),
            pltpu.SemaphoreType.DMA((count, 2 + span // LANES)),
            pltpu.SemaphoreType.DMA((count,)),
        ],
        compiler_params=pltpu.CompilerParams(vmem_limit_bytes=60 << 20),
    )(ix, gate, up, down)


def mix_kernel(pick_ref, rows_ref, gates_ref, half_ref, out_ref):
    tokens = gates_ref.shape[1]
    picked = dot(pick_ref[...], rows_ref[...])
    totals = [0.0, 0.0, 0.0]
    for k in range(2):
        gate = column(gates_ref[k : k + 1])
        for plane in range(3):
            start = (plane * 2 + k) * tokens
            one = picked[start : start + tokens]
            if plane == 2:
                one = jnp.where(half_ref[:, k : k + 1] > 0.5, one[:, 64:], one[:, :64])
            totals[plane] = totals[plane] + gate * one
    for plane in range(3):
        size = min(LANES, out_ref.shape[0] - plane * LANES)
        out_ref[plane * LANES : plane * LANES + size] = totals[plane].T.astype(BF)


def gate_up_kernel(
    ix_ref, rows_ref, gate_ref, up_ref, w1_ref, w2_ref, w3_ref, out_ref, g_ref, held, sems
):
    span = gate_ref.shape[0] // 4
    block = pl.multiple_of(ix_ref[0] * span, span)
    pairs = [
        (rows_ref, g_ref),
        (gate_ref.at[pl.ds(block, span)], held.at[0, pl.ds(0, span)]),
        (up_ref.at[pl.ds(block, span)], held.at[0, pl.ds(span, span)]),
    ]
    for s, w_ref in enumerate((w1_ref, w2_ref, w3_ref)):
        pairs.append((w_ref.at[pl.ds(0, 2 * span)], held.at[s + 1]))
    copies = [pltpu.make_async_copy(p, q, sems.at[n]) for n, (p, q) in enumerate(pairs)]
    for copy in copies:
        copy.start()
    copies[0].wait()
    rows = 2 * 192
    wide = [jnp.concatenate([g_ref[y, :rows], g_ref[y, rows : 2 * rows]], axis=1) for y in range(4)]
    slim = []
    for y in range(4):
        packed = g_ref[y, 2 * rows :]
        slim.append(jnp.concatenate([packed[:, :64], packed[:, 64:]], axis=0))
    pairs = [jnp.concatenate([slim[0], slim[1]], axis=1), jnp.concatenate([slim[2], slim[3]], axis=1)]
    copies[1].wait()
    for s in range(4):
        target = lax.rem(ix_ref[0] - s + 4, 4)
        copies[s + 2].wait()

        def weight(start, size):
            return jnp.concatenate(
                [held[s, start : start + size], held[s, span + start : span + start + size]], axis=1
            )

        total = dot(wide[0], weight(0, 256))
        for y in range(1, 4):
            total += dot(wide[y], weight(y * 320, 256))
        for p in range(2):
            low, high = weight(p * 640 + 256, 64), weight(p * 640 + 576, 64)
            total += dot(pairs[p], jnp.concatenate([low, high], axis=0))
        out_ref[target, :rows] = total[:, :LANES].astype(BF)
        out_ref[target, rows:] = total[:, LANES:].astype(BF)


def hidden_kernel(p_ref, out_ref):
    rows = p_ref.shape[1] // 2
    total = p_ref[0].astype(F32)
    for i in range(1, 4):
        total += p_ref[i].astype(F32)
    gate, up = total[:rows], total[rows:]
    hidden = (silu(gate) * up).astype(BF)
    for i in range(4):
        out_ref[i] = hidden


def down_kernel(ix_ref, rows_ref, down_ref, w1_ref, w2_ref, w3_ref, out_ref, h_ref, own_ref, held, sems):
    rows = h_ref.shape[1]
    half = rows // 2
    span = held.shape[1]
    block = pl.multiple_of(ix_ref[0] * span, span)
    pairs = [(rows_ref, h_ref), (down_ref.at[:, pl.ds(block, span)], own_ref)]
    for s, w_ref in enumerate((w1_ref, w2_ref, w3_ref)):
        pairs.append((w_ref.at[pl.ds(2 * span, span)], held.at[s]))
    copies = [pltpu.make_async_copy(p, q, sems.at[n]) for n, (p, q) in enumerate(pairs)]
    for copy in copies:
        copy.start()
    copies[0].wait()
    hid = [h_ref[lax.rem(ix_ref[0] - s + 4, 4)] for s in range(4)]

    def weight(s, start):
        if s == 0:
            return own_ref[:, start : start + 256]
        return jnp.concatenate(
            [held[s - 1, start : start + 128], held[s - 1, start + 128 : start + 256]], axis=1
        )

    full = 0.0
    for pair in ((0, 1), (2, 3)):
        for s in pair:
            copies[s + 1].wait()
        both = jnp.concatenate([hid[s] for s in pair], axis=1)
        full += jnp.concatenate(
            [
                dot(both, jnp.concatenate([weight(s, b * 256) for s in pair], axis=0))
                for b in range(span // 256)
            ],
            axis=1,
        )
    for y in range(4):
        own = full[:, y * 320 : (y + 1) * 320]
        out_ref[y, :rows] = own[:, :128].astype(BF)
        out_ref[y, rows : 2 * rows] = own[:, 128:256].astype(BF)
        last = own[:, 256:]
        out_ref[y, 2 * rows :] = jnp.concatenate([last[:half], last[half:]], axis=1).astype(BF)


def expert_call(kernel, shape, ix, operands, scratch):
    return pl.pallas_call(
        kernel,
        out_shape=jax.ShapeDtypeStruct(shape, BF),
        in_specs=[pl.BlockSpec(memory_space=pltpu.SMEM)]
        + [pl.BlockSpec(memory_space=pltpu.HBM)] * len(operands),
        out_specs=pl.BlockSpec(memory_space=pltpu.VMEM),
        scratch_shapes=scratch,
        compiler_params=pltpu.CompilerParams(vmem_limit_bytes=60 << 20),
    )(ix, *operands)


def body(
    seq_x,
    z_gate,
    bc_in,
    conv_x,
    conv_bc,
    log_decay,
    skip_d,
    norm_gain,
    routes,
    route_gates,
    placement,
    gate_w,
    up_w,
    down_w,
):
    tokens, width = seq_x.shape
    heads = width // HEAD_DIM
    experts = placement.shape[0]
    slots = experts * PIECE
    ix = lax.axis_index("x").astype(jnp.int32)
    place = jnp.stack([lax.axis_index(NEAR), lax.axis_index("c"), lax.axis_index("zh")]).astype(jnp.int32)

    edge = kernel_call(edge_kernel, [((16, 640), BF)], seq_x.T, bc_in)
    rim = lax.ppermute(edge, CTX, [(i, i + 1) for i in range(31)])
    ixs = ix.reshape(1)
    own = (gate_w[0], up_w[0], down_w[0])
    pieces = dict(zip((1, 3, 2), weight_pieces((1, 3, 2), ixs, *own)))
    swapped = {s: lax.ppermute(pieces[s], "x", [(i, (i + s) % 4) for i in range(4)]) for s in (1, 3)}
    xs, bcs, run, turn, message = kernel_call(
        state_kernel,
        [
            ((tokens, width), F32),
            ((tokens, 2 * STATE), F32),
            ((tokens, STATE), F32),
            ((STATE, tokens), F32),
            ((width + 16, STATE), BF),
        ],
        seq_x.T,
        bc_in,
        rim,
        conv_x,
        conv_bc,
        log_decay.T,
        scratch=[pltpu.VMEM((STATE, tokens), F32)],
    )
    near = lax.all_gather(message, NEAR)
    near, swapped[1], swapped[3] = lax.optimization_barrier((near, swapped[1], swapped[3]))
    near_carried, near_log, group = kernel_call(
        near_kernel,
        [((width, STATE), F32), ((8, STATE), F32), ((width // 2 + 16, STATE), BF)],
        place,
        near,
        scalars=1,
        scratch=[pltpu.VMEM((width, STATE), BF)],
    )
    fars = lax.all_gather(group, "zh")
    turn, group, *owned = lax.optimization_barrier((turn, group, routes, placement))
    select = kernel_call(
        select_kernel, [((slots, 4 * tokens), BF)], owned[0].T, owned[1].reshape(1, experts)
    )
    y_in, z_in = pl.pallas_call(
        inner_kernel,
        out_shape=[jax.ShapeDtypeStruct((tokens, width), F32)] * 2,
        in_specs=[pl.BlockSpec(memory_space=pltpu.VMEM)] * 4
        + [pl.BlockSpec(memory_space=pltpu.SMEM), pl.BlockSpec(memory_space=pltpu.VMEM)],
        out_specs=[pl.BlockSpec(memory_space=pltpu.VMEM)] * 2,
        compiler_params=pltpu.CompilerParams(vmem_limit_bytes=20 << 20),
    )(xs, bcs, run, turn, skip_d, z_gate.T)
    far = kernel_call(far_kernel, [((width // 2, STATE), BF)], place, fars, scalars=1)
    other = lax.ppermute(far, "c", [(0, 1), (1, 0)])
    normed, outgoing = kernel_call(
        finish_kernel,
        [((width, tokens), BF), ((slots, LANES), BF)],
        place,
        far,
        other,
        near_carried,
        near_log,
        bcs,
        run,
        y_in,
        z_in,
        norm_gain.reshape(1, width),
        select,
        scalars=1,
        scratch=[pltpu.VMEM((width, STATE), BF)],
    )
    normed, *own = lax.optimization_barrier((normed, routes, placement))
    swapped[2] = lax.ppermute(pieces[2], "x", [(i, (i + 2) % 4) for i in range(4)])
    pick, half = kernel_call(
        pick_kernel,
        [((6 * tokens, slots), BF), ((tokens, 2), F32)],
        own[0].T,
        own[1].reshape(1, experts),
    )
    arrived = lax.all_to_all(outgoing.reshape(experts, PIECE, LANES), CTX, 0, 0, tiled=True)
    rows = (
        arrived[:, : GROUPS * HALF]
        .reshape(experts, GROUPS, HALF, LANES)
        .transpose(1, 0, 2, 3)
        .reshape(GROUPS * experts * HALF, LANES)
    )
    wide = lax.all_gather(rows, "y")
    count = 2 * experts * HALF
    weights = [swapped[1], swapped[2], swapped[3]]
    span = gate_w.shape[1] // 4
    parts = []
    for start in range(0, width, LANES):
        stop = min(start + LANES, width)
        parts.append(conv(rim_ref[:, start:stop], turned(x_ref[start:stop]), cx_ref[:, start:stop]))
    xs = jnp.concatenate(parts, axis=1)
    bcs = conv(rim_ref[:, 384:], bc_ref[...].astype(F32), cbc_ref[...])
    lower = (iota((tokens, tokens), 0) >= iota((tokens, tokens), 1)).astype(F32)
    scratch[...] = jnp.zeros(scratch.shape, F32)
    scratch[:heads] = decay_ref[...]
    run = exact(lower, scratch[...], ((1,), (1,)))
    last = run[tokens - 1 : tokens]
    tails = jnp.exp(last - run)
    state = exact(xs * spread(tails, heads), bcs[:, :STATE], ((0,), (0,)))
    xs_ref[...] = xs
    bcs_ref[...] = bcs
    run_ref[...] = run
    turn_ref[...] = exact(scratch[...], lower, ((1,), (1,)))
    msg_ref[:width] = state.astype(BF)
    write_logs(msg_ref, width, last)


def inner_kernel(xs_ref, bcs_ref, run_ref, turn_ref, skip_ref, z_ref, y_ref, z_out_ref):
    tokens, width = xs_ref.shape
    lower = iota((tokens, tokens), 0) >= iota((tokens, tokens), 1)
    scores = exact(bcs_ref[:, STATE:], bcs_ref[:, :STATE], ((1,), (1,)))
    outs = []
    for h in range(width // HEAD_DIM):
        gaps = run_ref[:, h : h + 1] - turn_ref[h : h + 1]
        weight = jnp.where(lower, jnp.exp(jnp.where(lower, gaps, 0.0)), 0.0) * scores
        x = xs_ref[:, h * HEAD_DIM : (h + 1) * HEAD_DIM]
        outs.append(exact(weight, x) + skip_ref[h] * x)
    y_ref[...] = jnp.concatenate(outs, axis=1)
    z_out_ref[...] = silu(turned(z_ref[...]))


def near_kernel(place_ref, near_ref, carried_ref, log_ref, msg_ref, scratch):
    count, rows, _ = near_ref.shape
    rows -= 16
    heads = rows // HEAD_DIM
    total = [jnp.zeros((HEAD_DIM, STATE), F32)] * heads
    kept = total
    log = jnp.zeros((1, STATE), F32)
    kept_log = log
    for j in range(count):
        own = place_ref[0] == j
        kept = [jnp.where(own, t, k) for t, k in zip(total, kept)]
        kept_log = jnp.where(own, log, kept_log)
        step = read_logs(near_ref[j, rows:])
        factor = jnp.exp(step)
        log = log + step
        total = [
            factor[:, h : h + 1] * total[h] + near_ref[j, h * HEAD_DIM : (h + 1) * HEAD_DIM].astype(F32)
            for h in range(heads)
        ]
    for h in range(heads):
        carried_ref[h * HEAD_DIM : (h + 1) * HEAD_DIM] = kept[h]
        scratch[h * HEAD_DIM : (h + 1) * HEAD_DIM] = total[h].astype(BF)
    log_ref[...] = jnp.broadcast_to(kept_log, log_ref.shape)
    part = rows // 2
    msg_ref[:part] = scratch[pl.ds(pl.multiple_of(place_ref[1] * part, 32), part)]
    write_logs(msg_ref, part, log)


def far_kernel(place_ref, far_ref, out_ref):
    part = out_ref.shape[0]
    units = part // 32
    lanes = iota((1, STATE), 1)
    total = [jnp.zeros((32, STATE), F32)] * units
    for g in range(far_ref.shape[0] - 1):
        factor = jnp.exp(read_logs(far_ref[g, part:]))
        earlier = g < place_ref[2]
        for u in range(units):
            head = (place_ref[1] * units + u) // 2
            one = jnp.sum(jnp.where(lanes == head, factor, 0.0), axis=1, keepdims=True)
            state = far_ref[g, u * 32 : (u + 1) * 32].astype(F32)
            total[u] = jnp.where(earlier, one * total[u] + state, total[u])
    for u in range(units):
        out_ref[u * 32 : (u + 1) * 32] = total[u].astype(BF)


def finish_kernel(
    place_ref, own_ref, other_ref, near_ref, log_ref, bcs_ref, run_ref, y_ref, z_ref, gain_ref, select_ref,
    normed_ref, out_ref, scratch,
):
    part = own_ref.shape[0]
    tokens, width = y_ref.shape
    heads = width // HEAD_DIM
    core = place_ref[1]
    scratch[pl.ds(pl.multiple_of(core * part, 32), part)] = own_ref[...]
    scratch[pl.ds(pl.multiple_of((1 - core) * part, 32), part)] = other_ref[...]
    factor = jnp.exp(log_ref[0:1])
    carried = jnp.concatenate(
        [
            near_ref[h * HEAD_DIM : (h + 1) * HEAD_DIM]
            + factor[:, h : h + 1] * scratch[h * HEAD_DIM : (h + 1) * HEAD_DIM].astype(F32)
            for h in range(heads)
        ],
        axis=0,
    )
    outer = exact(bcs_ref[:, STATE:], carried, ((1,), (1,))) * spread(jnp.exp(run_ref[...]), heads)
    gated = (y_ref[...] + outer) * z_ref[...]
    square = gated * gated
    scales = jnp.concatenate(
        [
            jnp.broadcast_to(
                lax.rsqrt(
                    jnp.mean(square[:, h * HEAD_DIM : (h + 1) * HEAD_DIM], axis=1, keepdims=True) + 1e-05
                ),
                (tokens, HEAD_DIM),
            )
            for h in range(heads)
        ],
        axis=1,
    )
    normed = (gated * scales * gain_ref[...]).astype(BF)
    normed_ref[...] = turned(normed).astype(BF)
    blank = jnp.zeros((tokens, 64), BF)
    planes = jnp.concatenate(
        [
            normed[:, :128],
            normed[:, 128:256],
            jnp.concatenate([normed[:, 256:], blank], axis=1),
            jnp.concatenate([blank, normed[:, 256:]], axis=1),
        ],
        axis=0,
    )
    out_ref[...] = dot(select_ref[...], planes).astype(BF)


def piece_kernel(steps, ix_ref, gate_ref, up_ref, down_ref, *rest):
    outs, (held, in_sems, out_sems) = rest[: len(steps)], rest[len(steps) :]
    span = gate_ref.shape[0] // 4
    arrivals = []
    for i, step in enumerate(steps):
        block = pl.multiple_of(lax.rem(ix_ref[0] + step, 4) * span, span)
        pairs = [
            (gate_ref.at[pl.ds(block, span)], held.at[i, pl.ds(0, span)]),
            (up_ref.at[pl.ds(block, span)], held.at[i, pl.ds(span, span)]),
        ]
        for b in range(span // LANES):
            pairs.append(
                (
                    down_ref.at[:, pl.ds(pl.multiple_of(block + b * LANES, LANES), LANES)],
                    held.at[i, pl.ds(2 * span + b * LANES, LANES)],
                )
            )
        arrivals.append(
            [pltpu.make_async_copy(p, q, in_sems.at[i, n]) for n, (p, q) in enumerate(pairs)]
        )
    for copies in arrivals:
        for copy in copies:
            copy.start()
    departures = []
    for i, copies in enumerate(arrivals):
        for copy in copies:
            copy.wait()
        departures.append(pltpu.make_async_copy(held.at[i], outs[i], out_sems.at[i]))
        departures[i].start()
    for copy in departures:
        copy.wait()


def weight_pieces(steps, ix, gate, up, down):
    span = gate.shape[0] // 4
    count = len(steps)
    whole = pl.BlockSpec(memory_space=pltpu.HBM)
    return pl.pallas_call(
        functools.partial(piece_kernel, steps),
        out_shape=[jax.ShapeDtypeStruct((3 * span, LANES), BF)] * count,
        in_specs=[pl.BlockSpec(memory_space=pltpu.SMEM), whole, whole, whole],
        out_specs=[whole] * count,
        scratch_shapes=[
            pltpu.VMEM((count, 3 * span, LANES), BF),
            pltpu.SemaphoreType.DMA((count, 2 + span // LANES)),
            pltpu.SemaphoreType.DMA((count,)),
        ],
        compiler_params=pltpu.CompilerParams(vmem_limit_bytes=60 << 20),
    )(ix, gate, up, down)


def mix_kernel(pick_ref, rows_ref, gates_ref, half_ref, out_ref):
    tokens = gates_ref.shape[1]
    picked = dot(pick_ref[...], rows_ref[...])
    totals = [0.0, 0.0, 0.0]
    for k in range(2):
        gate = column(gates_ref[k : k + 1])
        for plane in range(3):
            start = (plane * 2 + k) * tokens
            one = picked[start : start + tokens]
            if plane == 2:
                one = jnp.where(half_ref[:, k : k + 1] > 0.5, one[:, 64:], one[:, :64])
            totals[plane] = totals[plane] + gate * one
    for plane in range(3):
        size = min(LANES, out_ref.shape[0] - plane * LANES)
        out_ref[plane * LANES : plane * LANES + size] = totals[plane].T.astype(BF)


def gate_up_kernel(
    ix_ref, rows_ref, gate_ref, up_ref, w1_ref, w2_ref, w3_ref, out_ref, g_ref, held, sems
):
    span = gate_ref.shape[0] // 4
    block = pl.multiple_of(ix_ref[0] * span, span)
    pairs = [
        (rows_ref, g_ref),
        (gate_ref.at[pl.ds(block, span)], held.at[0, pl.ds(0, span)]),
        (up_ref.at[pl.ds(block, span)], held.at[0, pl.ds(span, span)]),
    ]
    for s, w_ref in enumerate((w1_ref, w2_ref, w3_ref)):
        pairs.append((w_ref.at[pl.ds(0, 2 * span)], held.at[s + 1]))
    copies = [pltpu.make_async_copy(p, q, sems.at[n]) for n, (p, q) in enumerate(pairs)]
    for copy in copies:
        copy.start()
    copies[0].wait()
    rows = 2 * 192
    wide = [jnp.concatenate([g_ref[y, :rows], g_ref[y, rows : 2 * rows]], axis=1) for y in range(4)]
    slim = []
    for y in range(4):
        packed = g_ref[y, 2 * rows :]
        slim.append(jnp.concatenate([packed[:, :64], packed[:, 64:]], axis=0))
    pairs = [jnp.concatenate([slim[0], slim[1]], axis=1), jnp.concatenate([slim[2], slim[3]], axis=1)]
    copies[1].wait()
    for s in range(4):
        target = lax.rem(ix_ref[0] - s + 4, 4)
        copies[s + 2].wait()

        def weight(start, size):
            return jnp.concatenate(
                [held[s, start : start + size], held[s, span + start : span + start + size]], axis=1
            )

        total = dot(wide[0], weight(0, 256))
        for y in range(1, 4):
            total += dot(wide[y], weight(y * 320, 256))
        for p in range(2):
            low, high = weight(p * 640 + 256, 64), weight(p * 640 + 576, 64)
            total += dot(pairs[p], jnp.concatenate([low, high], axis=0))
        out_ref[target, :rows] = total[:, :LANES].astype(BF)
        out_ref[target, rows:] = total[:, LANES:].astype(BF)


def hidden_kernel(p_ref, out_ref):
    rows = p_ref.shape[1] // 2
    total = p_ref[0].astype(F32)
    for i in range(1, 4):
        total += p_ref[i].astype(F32)
    gate, up = total[:rows], total[rows:]
    hidden = (silu(gate) * up).astype(BF)
    for i in range(4):
        out_ref[i] = hidden


def down_kernel(ix_ref, rows_ref, down_ref, w1_ref, w2_ref, w3_ref, out_ref, h_ref, own_ref, held, sems):
    rows = h_ref.shape[1]
    half = rows // 2
    span = held.shape[1]
    block = pl.multiple_of(ix_ref[0] * span, span)
    pairs = [(rows_ref, h_ref), (down_ref.at[:, pl.ds(block, span)], own_ref)]
    for s, w_ref in enumerate((w1_ref, w2_ref, w3_ref)):
        pairs.append((w_ref.at[pl.ds(2 * span, span)], held.at[s]))
    copies = [pltpu.make_async_copy(p, q, sems.at[n]) for n, (p, q) in enumerate(pairs)]
    for copy in copies:
        copy.start()
    copies[0].wait()
    hid = [h_ref[lax.rem(ix_ref[0] - s + 4, 4)] for s in range(4)]

    def weight(s, start):
        if s == 0:
            return own_ref[:, start : start + 256]
        return jnp.concatenate(
            [held[s - 1, start : start + 128], held[s - 1, start + 128 : start + 256]], axis=1
        )

    full = 0.0
    for pair in ((0, 1), (2, 3)):
        for s in pair:
            copies[s + 1].wait()
        both = jnp.concatenate([hid[s] for s in pair], axis=1)
        full += jnp.concatenate(
            [
                dot(both, jnp.concatenate([weight(s, b * 256) for s in pair], axis=0))
                for b in range(span // 256)
            ],
            axis=1,
        )
    for y in range(4):
        own = full[:, y * 320 : (y + 1) * 320]
        out_ref[y, :rows] = own[:, :128].astype(BF)
        out_ref[y, rows : 2 * rows] = own[:, 128:256].astype(BF)
        last = own[:, 256:]
        out_ref[y, 2 * rows :] = jnp.concatenate([last[:half], last[half:]], axis=1).astype(BF)


def expert_call(kernel, shape, ix, operands, scratch):
    return pl.pallas_call(
        kernel,
        out_shape=jax.ShapeDtypeStruct(shape, BF),
        in_specs=[pl.BlockSpec(memory_space=pltpu.SMEM)]
        + [pl.BlockSpec(memory_space=pltpu.HBM)] * len(operands),
        out_specs=pl.BlockSpec(memory_space=pltpu.VMEM),
        scratch_shapes=scratch,
        compiler_params=pltpu.CompilerParams(vmem_limit_bytes=60 << 20),
    )(ix, *operands)


def body(
    seq_x,
    z_gate,
    bc_in,
    conv_x,
    conv_bc,
    log_decay,
    skip_d,
    norm_gain,
    routes,
    route_gates,
    placement,
    gate_w,
    up_w,
    down_w,
):
    tokens, width = seq_x.shape
    heads = width // HEAD_DIM
    experts = placement.shape[0]
    slots = experts * PIECE
    ix = lax.axis_index("x").astype(jnp.int32)
    place = jnp.stack([lax.axis_index(NEAR), lax.axis_index("c"), lax.axis_index("zh")]).astype(jnp.int32)

    edge = kernel_call(edge_kernel, [((16, 640), BF)], seq_x.T, bc_in)
    rim = lax.ppermute(edge, CTX, [(i, i + 1) for i in range(31)])
    ixs = ix.reshape(1)
    own = (gate_w[0], up_w[0], down_w[0])
    pieces = dict(zip((1, 3, 2), weight_pieces((1, 3, 2), ixs, *own)))
    swapped = {s: lax.ppermute(pieces[s], "x", [(i, (i + s) % 4) for i in range(4)]) for s in (1, 3)}
    xs, bcs, run, turn, message = kernel_call(
        state_kernel,
        [
            ((tokens, width), F32),
            ((tokens, 2 * STATE), F32),
            ((tokens, STATE), F32),
            ((STATE, tokens), F32),
            ((width + 16, STATE), BF),
        ],
        seq_x.T,
        bc_in,
        rim,
        conv_x,
        conv_bc,
        log_decay.T,
        scratch=[pltpu.VMEM((STATE, tokens), F32)],
    )
    near = lax.all_gather(message, NEAR)
    near, swapped[1], swapped[3] = lax.optimization_barrier((near, swapped[1], swapped[3]))
    near_carried, near_log, group = kernel_call(
        near_kernel,
        [((width, STATE), F32), ((8, STATE), F32), ((width // 2 + 16, STATE), BF)],
        place,
        near,
        scalars=1,
        scratch=[pltpu.VMEM((width, STATE), BF)],
    )
    fars = lax.all_gather(group, "zh")
    turn, group, *owned = lax.optimization_barrier((turn, group, routes, placement))
    select = kernel_call(
        select_kernel, [((slots, 4 * tokens), BF)], owned[0].T, owned[1].reshape(1, experts)
    )
    y_in, z_in = pl.pallas_call(
        inner_kernel,
        out_shape=[jax.ShapeDtypeStruct((tokens, width), F32)] * 2,
        in_specs=[pl.BlockSpec(memory_space=pltpu.VMEM)] * 4
        + [pl.BlockSpec(memory_space=pltpu.SMEM), pl.BlockSpec(memory_space=pltpu.VMEM)],
        out_specs=[pl.BlockSpec(memory_space=pltpu.VMEM)] * 2,
        compiler_params=pltpu.CompilerParams(vmem_limit_bytes=20 << 20),
    )(xs, bcs, run, turn, skip_d, z_gate.T)
    far = kernel_call(far_kernel, [((width // 2, STATE), BF)], place, fars, scalars=1)
    other = lax.ppermute(far, "c", [(0, 1), (1, 0)])
    normed, outgoing = kernel_call(
        finish_kernel,
        [((width, tokens), BF), ((slots, LANES), BF)],
        place,
        far,
        other,
        near_carried,
        near_log,
        bcs,
        run,
        y_in,
        z_in,
        norm_gain.reshape(1, width),
        select,
        scalars=1,
        scratch=[pltpu.VMEM((width, STATE), BF)],
    )
    normed, *own = lax.optimization_barrier((normed, routes, placement))
    swapped[2] = lax.ppermute(pieces[2], "x", [(i, (i + 2) % 4) for i in range(4)])
    pick, half = kernel_call(
        pick_kernel,
        [((6 * tokens, slots), BF), ((tokens, 2), F32)],
        own[0].T,
        own[1].reshape(1, experts),
    )
    arrived = lax.all_to_all(outgoing.reshape(experts, PIECE, LANES), CTX, 0, 0, tiled=True)
    rows = (
        arrived[:, : GROUPS * HALF]
        .reshape(experts, GROUPS, HALF, LANES)
        .transpose(1, 0, 2, 3)
        .reshape(GROUPS * experts * HALF, LANES)
    )
    wide = lax.all_gather(rows, "y")
    count = 2 * experts * HALF
    weights = [swapped[1], swapped[2], swapped[3]]
    span = gate_w.shape[1] // 4
    across = pl.BlockSpec((span, LANES), lambda i, b: (b[0], 0))
    along = pl.BlockSpec((LANES, span), lambda i, b: (0, b[0]))
    parts = expert_call(
        gate_up_kernel,
        (4, 2 * count, LANES),
        ixs,
        (wide, gate_w[0], up_w[0], *weights),
        [
            pltpu.VMEM(wide.shape, BF),
            pltpu.VMEM((4, 2 * span, LANES), BF),
            pltpu.SemaphoreType.DMA((6,)),
        ],
    )
    parts = lax.all_to_all(parts, "x", 0, 0, tiled=True)
    hidden = kernel_call(hidden_kernel, [((4, count, LANES), BF)], parts)
    hiddens = lax.all_to_all(hidden, "x", 0, 0, tiled=True)
    downs = expert_call(
        down_kernel,
        (4, count * 5 // 2, LANES),
        ixs,
        (hiddens, down_w[0], *weights),
        [
            pltpu.VMEM(hiddens.shape, BF),
            pltpu.VMEM((LANES, span), BF),
            pltpu.VMEM((3, span, LANES), BF),
            pltpu.SemaphoreType.DMA((5,)),
        ],
    )
    downs = lax.all_to_all(downs, "y", 0, 0, tiled=True)
    result = jnp.sum(downs.astype(F32), axis=0).astype(BF)
    result = result.reshape(GROUPS, experts, HALF, LANES).transpose(1, 0, 2, 3)
    result = jnp.pad(result.reshape(experts, GROUPS * HALF, LANES), ((0, 0), (0, 2), (0, 0)))
    returned = lax.all_to_all(result, CTX, 0, 0, tiled=True).reshape(slots, LANES)
    mixed = kernel_call(mix_kernel, [((width, tokens), BF)], pick, returned, route_gates.T, half)
    return (normed.T, mixed.T)


def solution(mesh):
    split = Mesh(mesh.devices.reshape(4, 4, 2, 4, 4), ("zh", "zl", "c", "x", "y"))
    placed = (
        P(CTX, EXP),
        P(CTX, EXP),
        P(CTX, None),
        P(None, EXP),
        P(),
        P(CTX, EXP),
        P(EXP),
        P(EXP),
        P(CTX, None),
        P(CTX, None),
        P(),
        P(CTX, None, EXP),
        P(CTX, None, EXP),
        P(CTX, EXP, None),
    )
    return jax.shard_map(
        body,
        mesh=split,
        in_specs=placed,
        out_specs=(P(CTX, EXP), P(CTX, EXP)),
        check_vma=False,
    )
```

```python
import functools

import jax
import jax.numpy as jnp
from jax import lax
from jax.experimental import pallas as pl
from jax.experimental.pallas import tpu as pltpu
from jax.sharding import Mesh
from jax.sharding import PartitionSpec as P

HEAD_DIM = 64
STATE = 128
CONV = 4
CTX = ("zh", "zl", "c")
EXP = ("x", "y")
NEAR = ("zl", "c")
LANES = 128
HALF = 6
GROUPS = 5
PIECE = 32

BF = jnp.bfloat16
F32 = jnp.float32


def dot(a, b):
    return jnp.dot(a, b, preferred_element_type=F32)


def kernel_call(kernel, outs, *operands, scalars=0, scratch=()):
    specs = [pl.BlockSpec(memory_space=pltpu.SMEM)] * scalars
    specs += [pl.BlockSpec(memory_space=pltpu.VMEM)] * (len(operands) - scalars)
    shapes = [jax.ShapeDtypeStruct(shape, kind) for shape, kind in outs]
    result = pl.pallas_call(
        kernel,
        out_shape=shapes,
        in_specs=specs,
        out_specs=[pl.BlockSpec(memory_space=pltpu.VMEM)] * len(outs),
        scratch_shapes=list(scratch),
        compiler_params=pltpu.CompilerParams(vmem_limit_bytes=20 << 20),
    )(*operands)
    return result[0] if len(outs) == 1 else result


def exact(a, b, dims=((1,), (0,))):
    return lax.dot_general(a, b, (dims, ((), ())), precision=lax.Precision.HIGHEST, preferred_element_type=F32)


def iota(shape, axis):
    return lax.broadcasted_iota(jnp.int32, shape, axis)


def silu(value):
    return value * jax.nn.sigmoid(value)


def turned(value):
    return value.astype(F32).T


def column(row):
    size = row.shape[1]
    hit = iota((size, size), 0) == iota((size, size), 1)
    return jnp.sum(jnp.where(hit, row.astype(F32), 0.0), axis=1, keepdims=True)


def edge_kernel(x_ref, bc_ref, out_ref):
    width, rows = x_ref.shape
    out_ref[:, :width] = turned(x_ref[...])[rows - 16 :].astype(BF)
    out_ref[:, width:384] = jnp.zeros((16, 384 - width), BF)
    out_ref[:, 384:] = bc_ref[rows - 16 :]


def pick_kernel(routes_ref, row_ref, pick_ref, half_ref):
    tokens = routes_ref.shape[1]
    experts = row_ref.shape[1]
    slots = experts * PIECE
    hot = [
        (column(routes_ref[k : k + 1]) == iota((tokens, experts), 1).astype(F32)).astype(F32)
        for k in range(2)
    ]
    earlier = (iota((tokens, tokens), 0) > iota((tokens, tokens), 1)).astype(BF)
    before = dot(earlier, (hot[0] + hot[1]).astype(BF))
    for k in range(2):
        rank = jnp.sum(hot[k] * before, axis=1, keepdims=True).astype(jnp.int32)
        owner = jnp.sum(hot[k] * row_ref[...].astype(F32), axis=1, keepdims=True).astype(jnp.int32)
        half = (rank >= HALF).astype(jnp.int32)
        base = owner * PIECE + rank - HALF * half
        half_ref[:, k : k + 1] = half.astype(F32)
        places = iota((tokens, slots), 1)
        for plane, where in enumerate((base + HALF * half, base + HALF * (half + 2), base + 4 * HALF)):
            start = (plane * 2 + k) * tokens
            pick_ref[start : start + tokens] = (places == where).astype(F32).astype(BF)


def select_kernel(routes_ref, row_ref, select_ref):
    tokens = routes_ref.shape[1]
    experts = row_ref.shape[1]
    slots = experts * PIECE
    hot = [(routes_ref[k : k + 1] == iota((experts, tokens), 0)).astype(F32) for k in range(2)]
    later = (iota((tokens, tokens), 0) < iota((tokens, tokens), 1)).astype(BF)
    before = dot((hot[0] + hot[1]).astype(BF), later)
    places = iota((slots, tokens), 0)
    planes = [jnp.zeros((slots, tokens), F32)] * 4
    owned = column(row_ref[...])
    for k in range(2):
        rank = jnp.sum(hot[k] * before, axis=0, keepdims=True).astype(jnp.int32)
        owner = jnp.sum(hot[k] * owned, axis=0, keepdims=True).astype(jnp.int32)
        half = (rank >= HALF).astype(jnp.int32)
        base = owner * PIECE + rank - HALF * half
        last = base + 4 * HALF
        wheres = (
            base + HALF * half,
            base + HALF * (half + 2),
            jnp.where(half == 0, last, -1),
            jnp.where(half == 1, last, -1),
        )
        planes = [p + (places == w).astype(F32) for p, w in zip(planes, wheres)]
    for plane in range(4):
        select_ref[:, plane * tokens : (plane + 1) * tokens] = planes[plane].astype(BF)


def spread(columns, heads):
    rows = columns.shape[0]
    return jnp.concatenate(
        [jnp.broadcast_to(columns[:, h : h + 1], (rows, HEAD_DIM)) for h in range(heads)], axis=1
    )


def write_logs(ref, start, logs):
    high = logs.astype(BF).astype(F32)
    places = iota((16, STATE), 0)
    tail = jnp.where(places == 0, high, jnp.where(places == 1, logs - high, 0.0))
    ref[start : start + 16] = tail.astype(BF)


def read_logs(tail):
    tail = tail.astype(F32)
    return tail[0:1] + tail[1:2]


def state_kernel(x_ref, bc_ref, rim_ref, cx_ref, cbc_ref, decay_ref, xs_ref, bcs_ref, run_ref, turn_ref, msg_ref, scratch):
    width, tokens = x_ref.shape
    heads = width // HEAD_DIM

    def conv(rim, value, taps):
        long = jnp.concatenate([rim.astype(F32), value], axis=0)
        total = taps[CONV - 1 : CONV] * long[16:]
        for back in range(1, CONV):
            total += taps[CONV - 1 - back : CONV - back] * pltpu.roll(long, back, 0)[16:]
        return silu(total)

    parts = []
    for start in range(0, width, LANES):
        stop = min(start + LANES, width)
        parts.append(conv(rim_ref[:, start:stop], turned(x_ref[start:stop]), cx_ref[:, start:stop]))
    xs = jnp.concatenate(parts, axis=1)
    bcs = conv(rim_ref[:, 384:], bc_ref[...].astype(F32), cbc_ref[...])
    lower = (iota((tokens, tokens), 0) >= iota((tokens, tokens), 1)).astype(F32)
    scratch[...] = jnp.zeros(scratch.shape, F32)
    scratch[:heads] = decay_ref[...]
    run = exact(lower, scratch[...], ((1,), (1,)))
    last = run[tokens - 1 : tokens]
    tails = jnp.exp(last - run)
    state = exact(xs * spread(tails, heads), bcs[:, :STATE], ((0,), (0,)))
    xs_ref[...] = xs
    bcs_ref[...] = bcs
    run_ref[...] = run
    turn_ref[...] = exact(scratch[...], lower, ((1,), (1,)))
    msg_ref[:width] = state.astype(BF)
    write_logs(msg_ref, width, last)


def inner_kernel(xs_ref, bcs_ref, run_ref, turn_ref, skip_ref, z_ref, y_ref, z_out_ref):
    tokens, width = xs_ref.shape
    lower = iota((tokens, tokens), 0) >= iota((tokens, tokens), 1)
    scores = exact(bcs_ref[:, STATE:], bcs_ref[:, :STATE], ((1,), (1,)))
    outs = []
    for h in range(width // HEAD_DIM):
        gaps = run_ref[:, h : h + 1] - turn_ref[h : h + 1]
        weight = jnp.where(lower, jnp.exp(jnp.where(lower, gaps, 0.0)), 0.0) * scores
        x = xs_ref[:, h * HEAD_DIM : (h + 1) * HEAD_DIM]
        outs.append(exact(weight, x) + skip_ref[h] * x)
    y_ref[...] = jnp.concatenate(outs, axis=1)
    z_out_ref[...] = silu(turned(z_ref[...]))


def near_kernel(place_ref, near_ref, carried_ref, log_ref, msg_ref, scratch):
    count, rows, _ = near_ref.shape
    rows -= 16
    heads = rows // HEAD_DIM
    total = [jnp.zeros((HEAD_DIM, STATE), F32)] * heads
    kept = total
    log = jnp.zeros((1, STATE), F32)
    kept_log = log
    for j in range(count):
        own = place_ref[0] == j
        kept = [jnp.where(own, t, k) for t, k in zip(total, kept)]
        kept_log = jnp.where(own, log, kept_log)
        step = read_logs(near_ref[j, rows:])
        factor = jnp.exp(step)
        log = log + step
        total = [
            factor[:, h : h + 1] * total[h] + near_ref[j, h * HEAD_DIM : (h + 1) * HEAD_DIM].astype(F32)
            for h in range(heads)
        ]
    for h in range(heads):
        carried_ref[h * HEAD_DIM : (h + 1) * HEAD_DIM] = kept[h]
        scratch[h * HEAD_DIM : (h + 1) * HEAD_DIM] = total[h].astype(BF)
    log_ref[...] = jnp.broadcast_to(kept_log, log_ref.shape)
    part = rows // 2
    msg_ref[:part] = scratch[pl.ds(pl.multiple_of(place_ref[1] * part, 32), part)]
    write_logs(msg_ref, part, log)


def far_kernel(place_ref, far_ref, out_ref):
    part = out_ref.shape[0]
    units = part // 32
    lanes = iota((1, STATE), 1)
    total = [jnp.zeros((32, STATE), F32)] * units
    for g in range(far_ref.shape[0] - 1):
        factor = jnp.exp(read_logs(far_ref[g, part:]))
        earlier = g < place_ref[2]
        for u in range(units):
            head = (place_ref[1] * units + u) // 2
            one = jnp.sum(jnp.where(lanes == head, factor, 0.0), axis=1, keepdims=True)
            state = far_ref[g, u * 32 : (u + 1) * 32].astype(F32)
            total[u] = jnp.where(earlier, one * total[u] + state, total[u])
    for u in range(units):
        out_ref[u * 32 : (u + 1) * 32] = total[u].astype(BF)


def finish_kernel(
    place_ref, own_ref, other_ref, near_ref, log_ref, bcs_ref, run_ref, y_ref, z_ref, gain_ref, select_ref,
    normed_ref, out_ref, scratch,
):
    part = own_ref.shape[0]
    tokens, width = y_ref.shape
    heads = width // HEAD_DIM
    core = place_ref[1]
    scratch[pl.ds(pl.multiple_of(core * part, 32), part)] = own_ref[...]
    scratch[pl.ds(pl.multiple_of((1 - core) * part, 32), part)] = other_ref[...]
    factor = jnp.exp(log_ref[0:1])
    carried = jnp.concatenate(
        [
            near_ref[h * HEAD_DIM : (h + 1) * HEAD_DIM]
            + factor[:, h : h + 1] * scratch[h * HEAD_DIM : (h + 1) * HEAD_DIM].astype(F32)
            for h in range(heads)
        ],
        axis=0,
    )
    outer = exact(bcs_ref[:, STATE:], carried, ((1,), (1,))) * spread(jnp.exp(run_ref[...]), heads)
    gated = (y_ref[...] + outer) * z_ref[...]
    square = gated * gated
    scales = jnp.concatenate(
        [
            jnp.broadcast_to(
                lax.rsqrt(
                    jnp.mean(square[:, h * HEAD_DIM : (h + 1) * HEAD_DIM], axis=1, keepdims=True) + 1e-05
                ),
                (tokens, HEAD_DIM),
            )
            for h in range(heads)
        ],
        axis=1,
    )
    normed = (gated * scales * gain_ref[...]).astype(BF)
    normed_ref[...] = turned(normed).astype(BF)
    blank = jnp.zeros((tokens, 64), BF)
    planes = jnp.concatenate(
        [
            normed[:, :128],
            normed[:, 128:256],
            jnp.concatenate([normed[:, 256:], blank], axis=1),
            jnp.concatenate([blank, normed[:, 256:]], axis=1),
        ],
        axis=0,
    )
    out_ref[...] = dot(select_ref[...], planes).astype(BF)


def piece_kernel(steps, ix_ref, gate_ref, up_ref, down_ref, *rest):
    outs, (held, in_sems, out_sems) = rest[: len(steps)], rest[len(steps) :]
    span = gate_ref.shape[0] // 4
    arrivals = []
    for i, step in enumerate(steps):
        block = pl.multiple_of(lax.rem(ix_ref[0] + step, 4) * span, span)
        pairs = [
            (gate_ref.at[pl.ds(block, span)], held.at[i, pl.ds(0, span)]),
            (up_ref.at[pl.ds(block, span)], held.at[i, pl.ds(span, span)]),
        ]
        for b in range(span // LANES):
            pairs.append(
                (
                    down_ref.at[:, pl.ds(pl.multiple_of(block + b * LANES, LANES), LANES)],
                    held.at[i, pl.ds(2 * span + b * LANES, LANES)],
                )
            )
        arrivals.append(
            [pltpu.make_async_copy(p, q, in_sems.at[i, n]) for n, (p, q) in enumerate(pairs)]
        )
    for copies in arrivals:
        for copy in copies:
            copy.start()
    departures = []
    for i, copies in enumerate(arrivals):
        for copy in copies:
            copy.wait()
        departures.append(pltpu.make_async_copy(held.at[i], outs[i], out_sems.at[i]))
        departures[i].start()
    for copy in departures:
        copy.wait()


def weight_pieces(steps, ix, gate, up, down):
    span = gate.shape[0] // 4
    count = len(steps)
    whole = pl.BlockSpec(memory_space=pltpu.HBM)
    return pl.pallas_call(
        functools.partial(piece_kernel, steps),
        out_shape=[jax.ShapeDtypeStruct((3 * span, LANES), BF)] * count,
        in_specs=[pl.BlockSpec(memory_space=pltpu.SMEM), whole, whole, whole],
        out_specs=[whole] * count,
        scratch_shapes=[
            pltpu.VMEM((count, 3 * span, LANES), BF),
            pltpu.SemaphoreType.DMA((count, 2 + span // LANES)),
            pltpu.SemaphoreType.DMA((count,)),
        ],
        compiler_params=pltpu.CompilerParams(vmem_limit_bytes=60 << 20),
    )(ix, gate, up, down)


def mix_kernel(pick_ref, rows_ref, gates_ref, half_ref, out_ref):
    tokens = gates_ref.shape[1]
    picked = dot(pick_ref[...], rows_ref[...])
    totals = [0.0, 0.0, 0.0]
    for k in range(2):
        gate = column(gates_ref[k : k + 1])
        for plane in range(3):
            start = (plane * 2 + k) * tokens
            one = picked[start : start + tokens]
            if plane == 2:
                one = jnp.where(half_ref[:, k : k + 1] > 0.5, one[:, 64:], one[:, :64])
            totals[plane] = totals[plane] + gate * one
    for plane in range(3):
        size = min(LANES, out_ref.shape[0] - plane * LANES)
        out_ref[plane * LANES : plane * LANES + size] = totals[plane].T.astype(BF)


def gate_up_kernel(ix_ref, g_ref, w0_ref, w1_ref, w2_ref, w3_ref, out_ref):
    rows = 2 * 192
    wide = [jnp.concatenate([g_ref[y, :rows], g_ref[y, rows : 2 * rows]], axis=1) for y in range(4)]
    slim = []
    for y in range(4):
        packed = g_ref[y, 2 * rows :]
        slim.append(jnp.concatenate([packed[:, :64], packed[:, 64:]], axis=0))
    pairs = [jnp.concatenate([slim[0], slim[1]], axis=1), jnp.concatenate([slim[2], slim[3]], axis=1)]
    for s, w_ref in enumerate((w0_ref, w1_ref, w2_ref, w3_ref)):
        target = lax.rem(ix_ref[0] - s + 4, 4)

        def weight(start, size):
            return jnp.concatenate(
                [w_ref[start : start + size], w_ref[1280 + start : 1280 + start + size]], axis=1
            )

        total = dot(wide[0], weight(0, 256))
        for y in range(1, 4):
            total += dot(wide[y], weight(y * 320, 256))
        for p in range(2):
            low, high = weight(p * 640 + 256, 64), weight(p * 640 + 576, 64)
            total += dot(pairs[p], jnp.concatenate([low, high], axis=0))
        out_ref[target, :rows] = total[:, :LANES].astype(BF)
        out_ref[target, rows:] = total[:, LANES:].astype(BF)


def hidden_kernel(p_ref, out_ref):
    rows = p_ref.shape[1] // 2
    total = p_ref[0].astype(F32)
    for i in range(1, 4):
        total += p_ref[i].astype(F32)
    gate, up = total[:rows], total[rows:]
    hidden = (silu(gate) * up).astype(BF)
    for i in range(4):
        out_ref[i] = hidden


def down_kernel(ix_ref, h_ref, w0_ref, w1_ref, w2_ref, w3_ref, out_ref):
    rows = h_ref.shape[1]
    half = rows // 2
    hid = jnp.concatenate([h_ref[lax.rem(ix_ref[0] - s + 4, 4)] for s in range(4)], axis=1)
    blocks = []
    for b in range(5):
        weight = []
        for w_ref in (w0_ref, w1_ref, w2_ref, w3_ref):
            start = b * 256
            weight.append(
                jnp.concatenate([w_ref[start : start + 128], w_ref[start + 128 : start + 256]], axis=1)
            )
        blocks.append(dot(hid, jnp.concatenate(weight, axis=0)))
    full = jnp.concatenate(blocks, axis=1)
    for y in range(4):
        own = full[:, y * 320 : (y + 1) * 320]
        out_ref[y, :rows] = own[:, :128].astype(BF)
        out_ref[y, rows : 2 * rows] = own[:, 128:256].astype(BF)
        last = own[:, 256:]
        out_ref[y, 2 * rows :] = jnp.concatenate([last[:half], last[half:]], axis=1).astype(BF)


def expert_call(kernel, shape, ix, rows, pieces, piece_spec):
    return pl.pallas_call(
        kernel,
        out_shape=jax.ShapeDtypeStruct(shape, BF),
        grid_spec=pltpu.PrefetchScalarGridSpec(
            num_scalar_prefetch=1,
            grid=(1,),
            in_specs=[pl.BlockSpec(rows.shape, lambda i, b: (0, 0, 0))] + [piece_spec] * len(pieces),
            out_specs=pl.BlockSpec(shape, lambda i, b: (0, 0, 0)),
        ),
        compiler_params=pltpu.CompilerParams(vmem_limit_bytes=20 << 20),
    )(ix, rows, *pieces)


def body(
    seq_x,
    z_gate,
    bc_in,
    conv_x,
    conv_bc,
    log_decay,
    skip_d,
    norm_gain,
    routes,
    route_gates,
    placement,
    gate_w,
    up_w,
    down_w,
):
    tokens, width = seq_x.shape
    heads = width // HEAD_DIM
    experts = placement.shape[0]
    slots = experts * PIECE
    ix = lax.axis_index("x").astype(jnp.int32)
    place = jnp.stack([lax.axis_index(NEAR), lax.axis_index("c"), lax.axis_index("zh")]).astype(jnp.int32)

    edge = kernel_call(edge_kernel, [((16, 640), BF)], seq_x.T, bc_in)
    ixs, edge = lax.optimization_barrier((ix.reshape(1), edge))
    rim = lax.ppermute(edge, CTX, [(i, i + 1) for i in range(31)])
    own = (gate_w[0], up_w[0], down_w[0])
    pieces = dict(zip((1, 3, 2, 0), weight_pieces((1, 3, 2, 0), ixs, *own)))
    swapped = {s: lax.ppermute(pieces[s], "x", [(i, (i + s) % 4) for i in range(4)]) for s in (1, 3)}
    xs, bcs, run, turn, message = kernel_call(
        state_kernel,
        [
            ((tokens, width), F32),
            ((tokens, 2 * STATE), F32),
            ((tokens, STATE), F32),
            ((STATE, tokens), F32),
            ((width + 16, STATE), BF),
        ],
        seq_x.T,
        bc_in,
        rim,
        conv_x,
        conv_bc,
        log_decay.T,
        scratch=[pltpu.VMEM((STATE, tokens), F32)],
    )
    near = lax.all_gather(message, NEAR)
    near, swapped[1], swapped[3] = lax.optimization_barrier((near, swapped[1], swapped[3]))
    near_carried, near_log, group = kernel_call(
        near_kernel,
        [((width, STATE), F32), ((8, STATE), F32), ((width // 2 + 16, STATE), BF)],
        place,
        near,
        scalars=1,
        scratch=[pltpu.VMEM((width, STATE), BF)],
    )
    fars = lax.all_gather(group, "zh")
    turn, group, *owned = lax.optimization_barrier((turn, group, routes, placement))
    select = kernel_call(
        select_kernel, [((slots, 4 * tokens), BF)], owned[0].T, owned[1].reshape(1, experts)
    )
    y_in, z_in = pl.pallas_call(
        inner_kernel,
        out_shape=[jax.ShapeDtypeStruct((tokens, width), F32)] * 2,
        in_specs=[pl.BlockSpec(memory_space=pltpu.VMEM)] * 4
        + [pl.BlockSpec(memory_space=pltpu.SMEM), pl.BlockSpec(memory_space=pltpu.VMEM)],
        out_specs=[pl.BlockSpec(memory_space=pltpu.VMEM)] * 2,
        compiler_params=pltpu.CompilerParams(vmem_limit_bytes=20 << 20),
    )(xs, bcs, run, turn, skip_d, z_gate.T)
    far = kernel_call(far_kernel, [((width // 2, STATE), BF)], place, fars, scalars=1)
    other = lax.ppermute(far, "c", [(0, 1), (1, 0)])
    normed, outgoing = kernel_call(
        finish_kernel,
        [((width, tokens), BF), ((slots, LANES), BF)],
        place,
        far,
        other,
        near_carried,
        near_log,
        bcs,
        run,
        y_in,
        z_in,
        norm_gain.reshape(1, width),
        select,
        scalars=1,
        scratch=[pltpu.VMEM((width, STATE), BF)],
    )
    normed, *own = lax.optimization_barrier((normed, routes, placement))
    swapped[2] = lax.ppermute(pieces[2], "x", [(i, (i + 2) % 4) for i in range(4)])
    pick, half = kernel_call(
        pick_kernel,
        [((6 * tokens, slots), BF), ((tokens, 2), F32)],
        own[0].T,
        own[1].reshape(1, experts),
    )
    arrived = lax.all_to_all(outgoing.reshape(experts, PIECE, LANES), CTX, 0, 0, tiled=True)
    rows = (
        arrived[:, : GROUPS * HALF]
        .reshape(experts, GROUPS, HALF, LANES)
        .transpose(1, 0, 2, 3)
        .reshape(GROUPS * experts * HALF, LANES)
    )
    wide = lax.all_gather(rows, "y")
    count = 2 * experts * HALF
    weights = [pieces[0], swapped[1], swapped[2], swapped[3]]
    parts = expert_call(
        gate_up_kernel,
        (4, 2 * count, LANES),
        ixs,
        wide,
        weights,
        pl.BlockSpec((2 * gate_w.shape[1] // 4, LANES), lambda i, b: (0, 0)),
    )
    parts = lax.all_to_all(parts, "x", 0, 0, tiled=True)
    hidden = kernel_call(hidden_kernel, [((4, count, LANES), BF)], parts)
    hiddens = lax.all_to_all(hidden, "x", 0, 0, tiled=True)
    downs = expert_call(
        down_kernel,
        (4, count * 5 // 2, LANES),
        ixs,
        hiddens,
        weights,
        pl.BlockSpec((gate_w.shape[1] // 4, LANES), lambda i, b: (2, 0)),
    )
    downs = lax.all_to_all(downs, "y", 0, 0, tiled=True)
    result = jnp.sum(downs.astype(F32), axis=0).astype(BF)
    result = result.reshape(GROUPS, experts, HALF, LANES).transpose(1, 0, 2, 3)
    result = jnp.pad(result.reshape(experts, GROUPS * HALF, LANES), ((0, 0), (0, 2), (0, 0)))
    returned = lax.all_to_all(result, CTX, 0, 0, tiled=True).reshape(slots, LANES)
    mixed = kernel_call(mix_kernel, [((width, tokens), BF)], pick, returned, route_gates.T, half)
    return (normed.T, mixed.T)


def solution(mesh):
    split = Mesh(mesh.devices.reshape(4, 4, 2, 4, 4), ("zh", "zl", "c", "x", "y"))
    placed = (
        P(CTX, EXP),
        P(CTX, EXP),
        P(CTX, None),
        P(None, EXP),
        P(),
        P(CTX, EXP),
        P(EXP),
        P(EXP),
        P(CTX, None),
        P(CTX, None),
        P(),
        P(CTX, None, EXP),
        P(CTX, None, EXP),
        P(CTX, EXP, None),
    )
    return jax.shard_map(
        body,
        mesh=split,
        in_specs=placed,
        out_specs=(P(CTX, EXP), P(CTX, EXP)),
        check_vma=False,
    )
```
